256 devices in a mesh: slab: 128 (over y, z, x), blk: 2 (over core).
Axes of the slice: x: 4, y: 4, z: 8, core: 2. Of those that a mesh axis runs over, the one named last changes fastest.
Arguments:
- slip_rate: float32 [262144], P('slab'), may hold values from 0.1 to 3
- log_state: float32 [262144], P('slab'), may hold values from -1 to 1
- friction_a: float32 [262144], P('slab'), may hold values from 0.2 to 1
- friction_b: float32 [262144], P('slab'), may hold values from 0.2 to 1
- normal_stress: float32 [262144], P('slab'), may hold values from 2 to 4
- leak_rate: float32 [262144], P('slab'), may hold values from 0.5 to 2
- corner: int32 [3, 262144], P(None, 'slab'), may hold values from 0 to 1022, as said below
- fraction: float32 [3, 262144], P(None, 'slab'), may hold values from 0 to 1
- near_blocks: bfloat16 [512, 3, 512, 512], P(('slab', 'blk')), may hold values from -0.15625 to 0.15625
- row_basis: bfloat16 [24, 262144], P(None, 'slab'), may hold values from -1.25 to 1.25
- col_basis: bfloat16 [24, 262144], P(None, 'slab'), may hold values from -0.25 to 0.25
- far_row: int32 [262144], P(('slab', 'blk')), may hold values from 0 to 3
- far_col: int32 [262144], P(('slab', 'blk')), may hold values from 0 to 511, as said below
- far_rank: int32 [262144], P(('slab', 'blk')), may hold values from 0 to 24, as said below
- far_coupling: bfloat16 [24, 24, 262144], P(None, None, ('slab', 'blk')), may hold values from -0.078125 to 0.078125
- pressure: float32 [256, 512, 1024], P('slab', 'blk'), may hold values from -1 to 1
- region: int32 [256, 512, 1024], P('slab', 'blk'), may hold values from 0 to 15
- perm_table: float32 [16], replicated, may hold values from 0.05 to 1
Outputs:
- slip_accel: float32 [262144], P('slab')
- state_rate: float32 [262144], P('slab')
- pressure_rate: float32 [256, 512, 1024], P('slab', 'blk')
The draws below stay inside these ranges and needn't reach their ends.
Inputs may be any that keep to these rules, and one draw needn't show every extreme that they name: corner[0, f] equals 2 * (f // 2048), the first plane of the slab that holds cell f; corner[1, f] is at most 510 and corner[2, f] at most 1022. far_col[s] differs by 2 or more (cyclically over 512 clusters) from the slot's row cluster 4 * (s // 2048) + far_row[s]. `far_rank`: slots with rank 0 are empty; the live slots of a device come first, and some device has all 1024 slots live.
All inputs are finite; a program needn't handle non-finite values.
Results may differ from the reference program's by a relative error of at most 0.0022.
Values may be sent and summed in bfloat16 or wider, within the bound.
A program may use at most 64 MiB of HBM per device.

```python
import math
import jax
import jax.numpy as jnp
from jax import lax

CS = 512
RANK = 24
REGIONS = 16
CL = 4
FB = 1024
CX = 2
CY = 256
CZ = 1024
C = 512
FAULT = 262144
SLOTS = 262144
NX = 256
NY = 512
NZ = 1024
N_SLAB = 128
N_BLK = 2


def far_slots(key):
    total = N_SLAB * N_BLK * FB
    clusters = CL * N_SLAB
    slot = jnp.arange(total, dtype=jnp.int32)
    owner = slot // FB
    rows = jax.random.randint(jax.random.fold_in(key, 11), (total,), 0, CL)
    global_row = owner // N_BLK * CL + rows
    offset = jax.random.randint(jax.random.fold_in(key, 12), (total,), 0, clusters - 3)
    cols = (global_row + 2 + offset) % clusters
    return (rows.astype(jnp.int32), cols.astype(jnp.int32))


def draw_far_row(key, part):
    return far_slots(key)[0]


def draw_far_col(key, part):
    return far_slots(key)[1]


def draw_far_rank(key, part):
    devices = N_SLAB * N_BLK
    total = devices * FB
    slot = jnp.arange(total, dtype=jnp.int32)
    live = jax.random.randint(jax.random.fold_in(key, 13), (devices,), FB // 8, FB + 1)
    chosen = jax.random.randint(jax.random.fold_in(key, 15), (), 0, devices)
    live = jnp.where(jnp.arange(devices, dtype=jnp.int32) == chosen, FB, live)
    ranks = jax.random.randint(jax.random.fold_in(key, 14), (total,), 1, RANK + 1)
    return jnp.where(slot % FB < live[slot // FB], ranks, 0).astype(jnp.int32)


def draw_corner(key, part):
    cells = CL * N_SLAB * CS
    position = jnp.arange(cells, dtype=jnp.int32)
    slab_group = position // (CL * CS)
    first = slab_group * CX + jax.random.randint(jax.random.fold_in(key, 21), (cells,), 0, CX - 1)
    second = jax.random.randint(jax.random.fold_in(key, 22), (cells,), 0, CY * N_BLK - 1)
    third = jax.random.randint(jax.random.fold_in(key, 23), (cells,), 0, CZ - 1)
    return jnp.stack([first, second, third]).astype(jnp.int32)


def set_ends(result, key, low, top_value):
    longest = result.shape.index(max(result.shape))
    spots = []
    for shift in (0, 1):
        where = [jax.random.randint(jax.random.fold_in(key, axis), (), 0, length) for axis, length in enumerate(result.shape)]
        where[longest] = (where[longest] + shift) % result.shape[longest]
        spots.append(tuple(where))
    return result.at[spots[0]].set(low).at[spots[1]].set(top_value)


def shard_levels(stream_key, shape, shards, smallest, top_value):
    factor_of, own = 1.0, jax.random.fold_in(stream_key, 6)
    for axis_at, shards_of in shards:
        heights = jnp.exp(jax.random.uniform(jax.random.fold_in(own, axis_at), (shards_of,), jnp.float32, smallest / len(shards), top_value / len(shards)))
        factor_of = factor_of * jnp.repeat(heights, shape[axis_at] // shards_of).reshape([-1 if axis == axis_at else 1 for axis in range(len(shape))])
    return factor_of


def gaussian(key, dims, scale, reach, cuts=(), kind=jnp.bfloat16):
    entries = scale * jax.random.normal(key, dims, jnp.float32)
    if cuts:
        entries = entries * shard_levels(key, dims, cuts, -0.22, 0.18)
    return jnp.clip(entries, -reach, reach).astype(kind)


def setup_inputs(seed: int = 0) -> dict:
    keys = jax.random.split(jax.random.key(seed), 19)
    return {
        "slip_rate": jnp.clip(jnp.exp(math.log(3.0) - 3.4011974 * jax.random.uniform(keys[0], (FAULT,), jnp.float32) ** shard_levels(keys[0], (FAULT,), ((0, 128),), -0.2, 0.2)), 0.1, 3.0),
        "log_state": jnp.clip(jax.random.uniform(keys[1], (FAULT,), jnp.float32, -1.0, 1.0) * shard_levels(keys[1], (FAULT,), ((0, 128),), -0.4, 0.0), -1.0, 1.0),
        "friction_a": jnp.clip(jnp.exp(math.log(1.0) - 1.609438 * jax.random.uniform(keys[2], (FAULT,), jnp.float32) ** shard_levels(keys[2], (FAULT,), ((0, 128),), -0.2, 0.2)), 0.2, 1.0),
        "friction_b": jnp.clip(jnp.exp(math.log(1.0) - 1.609438 * jax.random.uniform(keys[3], (FAULT,), jnp.float32) ** shard_levels(keys[3], (FAULT,), ((0, 128),), -0.2, 0.2)), 0.2, 1.0),
        "normal_stress": jnp.clip(2.0 + 2.0 * jax.random.uniform(keys[4], (FAULT,), jnp.float32) ** shard_levels(keys[4], (FAULT,), ((0, 128),), -0.2, 0.2), 2.0, 4.0),
        "leak_rate": jnp.clip(jnp.exp(math.log(2.0) - 1.3862944 * jax.random.uniform(keys[5], (FAULT,), jnp.float32) ** shard_levels(keys[5], (FAULT,), ((0, 128),), -0.2, 0.2)), 0.5, 2.0),
        "corner": draw_corner(jax.random.fold_in(keys[18], 71), 0),
        "fraction": jnp.clip(1.0 * jax.random.uniform(keys[7], (3, FAULT), jnp.float32) ** shard_levels(keys[7], (3, FAULT), ((1, 128),), -0.2, 0.2), 0.0, 1.0),
        "near_blocks": gaussian(keys[8], (C, 3, CS, CS), (3 * CS) ** -0.5, 0.15625, ((0, 256),)),
        "row_basis": gaussian(keys[9], (RANK, FAULT), RANK ** -0.5, 1.25, ((1, 128),)),
        "col_basis": gaussian(keys[10], (RANK, FAULT), CS ** -0.5, 0.25, ((1, 128),)),
        "far_row": draw_far_row(jax.random.fold_in(keys[18], 71), 0),
        "far_col": draw_far_col(jax.random.fold_in(keys[18], 71), 0),
        "far_rank": draw_far_rank(jax.random.fold_in(keys[18], 71), 0),
        "far_coupling": gaussian(keys[14], (RANK, RANK, SLOTS), (RANK * FB * N_BLK // (2 * CL)) ** -0.5, 0.078125, ((2, 256),)),
        "pressure": gaussian(keys[15], (NX, NY, NZ), 0.25, 1.0, ((0, 128), (1, 2)), jnp.float32),
        "region": set_ends(jax.random.randint(keys[16], (NX, NY, NZ), 0, REGIONS), jax.random.fold_in(keys[16], 1), 0, REGIONS - 1).astype(jnp.int32),
        "perm_table": jnp.clip(jnp.exp(jax.random.uniform(keys[17], (REGIONS,), jnp.float32, math.log(0.05), math.log(1.0))), 0.05, 1.0),
    }


def corner_list(corner, fraction):
    listed = []
    for shift_x in (0, 1):
        for shift_y in (0, 1):
            for shift_z in (0, 1):
                factor_x = fraction[0] if shift_x else 1.0 - fraction[0]
                factor_y = fraction[1] if shift_y else 1.0 - fraction[1]
                factor_z = fraction[2] if shift_z else 1.0 - fraction[2]
                weight = factor_x * factor_y * factor_z
                listed.append((corner[0] + shift_x, corner[1] + shift_y, corner[2] + shift_z, weight))
    return listed


def stencil(padded_p, padded_k):
    centre_p = padded_p[1:-1, 1:-1, 1:-1]
    centre_k = padded_k[1:-1, 1:-1, 1:-1]
    summed = jnp.zeros_like(centre_p)
    for slices in ((slice(2, None), slice(1, -1), slice(1, -1)), (slice(0, -2), slice(1, -1), slice(1, -1)),
                   (slice(1, -1), slice(2, None), slice(1, -1)), (slice(1, -1), slice(0, -2), slice(1, -1)),
                   (slice(1, -1), slice(1, -1), slice(2, None)), (slice(1, -1), slice(1, -1), slice(0, -2))):
        other_k = padded_k[slices]
        other_p = padded_p[slices]
        summed = summed + 2.0 * centre_k * other_k / (centre_k + other_k) * (other_p - centre_p)
    return summed


def reference(slip_rate, log_state, friction_a, friction_b, normal_stress, leak_rate, corner, fraction,
              near_blocks, row_basis, col_basis, far_row, far_col, far_rank, far_coupling, pressure, region,
              perm_table):
    slip_low = slip_rate.astype(jnp.bfloat16)
    by_cluster = jnp.pad(slip_low.reshape(C, CS), ((1, 1), (0, 0)))

    def near_row(which):
        window = lax.dynamic_slice_in_dim(by_cluster, which, 3, 0).astype(jnp.float32)
        blocks = near_blocks[which].astype(jnp.float32)
        return jnp.einsum('jxy,jy->x', blocks, window)

    near_traction = lax.map(near_row, jnp.arange(C, dtype=jnp.int32))
    moments = jnp.einsum('acx,cx->ac', col_basis.reshape(RANK, C, CS).astype(jnp.float32),
                         slip_low.reshape(C, CS).astype(jnp.float32),
                         precision=lax.Precision.HIGHEST).astype(jnp.bfloat16)
    ranks_iota = lax.broadcasted_iota(jnp.int32, (RANK, FB), 0)
    cluster_iota = lax.broadcasted_iota(jnp.int32, (C, FB), 0)

    def add_device(totals, device):
        start = (device * FB).astype(jnp.int32)
        coupling = lax.dynamic_slice_in_dim(far_coupling, start, FB, 2).astype(jnp.float32)
        cols = lax.dynamic_slice_in_dim(far_col, start, FB, 0)
        rows = lax.dynamic_slice_in_dim(far_row, start, FB, 0)
        ranks = lax.dynamic_slice_in_dim(far_rank, start, FB, 0)
        picked = jnp.take(moments, cols, axis=1).astype(jnp.float32)
        masked = jnp.where(ranks_iota < ranks[None, :], picked, jnp.float32(0.0))
        block = jnp.einsum('akf,kf->af', coupling, masked)
        global_row = (device // N_BLK).astype(jnp.int32) * CL + rows
        one_hot = (global_row[None, :] == cluster_iota).astype(jnp.float32)
        return totals + jnp.dot(block, one_hot.T, precision=lax.Precision.HIGHEST), None

    totals, _ = lax.scan(add_device, jnp.zeros((RANK, C), jnp.float32),
                         jnp.arange(N_SLAB * N_BLK, dtype=jnp.int32))
    far_traction = jnp.einsum('acx,ac->cx', row_basis.reshape(RANK, C, CS).astype(jnp.float32), totals,
                              precision=lax.Precision.HIGHEST)
    traction = (near_traction + far_traction).reshape(FAULT)

    listed = corner_list(corner, fraction)
    fault_pressure = jnp.zeros((FAULT,), jnp.float32)
    source = jnp.zeros((NX, NY, NZ), jnp.float32)
    flow = leak_rate * slip_rate
    for place_x, place_y, place_z, weight in listed:
        fault_pressure = fault_pressure + weight * pressure[place_x, place_y, place_z]
        source = source.at[place_x, place_y, place_z].add(weight * flow)
    effective = normal_stress - fault_pressure
    state_rate = jnp.exp(-log_state) - slip_rate
    slip_accel = (traction - effective * friction_b * state_rate) / (effective * friction_a / slip_rate + 0.5)

    permeability = jnp.zeros((NX, NY, NZ), jnp.float32)
    for which in range(REGIONS):
        permeability = jnp.where(region == which, perm_table[which], permeability)
    padded_p = jnp.pad(pressure, 1)
    padded_k = jnp.pad(permeability, 1)
    pressure_rate = source + stencil(padded_p, padded_k)
    return slip_accel, state_rate, pressure_rate
```

```python
import functools

import jax
import jax.numpy as jnp
from jax import lax
from jax.experimental import pallas as pl
from jax.experimental.pallas import tpu as pltpu
from jax.sharding import Mesh
from jax.sharding import PartitionSpec as P

SLAB = ("slab_0", "slab_1", "slab_2")
SLAB_BLK = ("slab_0", "slab_1", "slab_2", "blk")
MESH = pl.DeviceIdType.MESH

PARTS = 4
F_TILE = 256
HALO = 8
FAR = 1e30


def lanes_row(ref, first, count):
    return jnp.concatenate([ref[first + q : first + q + 1, :] for q in range(count)], axis=1)


def store_rows(ref, first, row):
    for q in range(row.shape[1] // 128):
        ref[first + q : first + q + 1, :] = row[:, 128 * q : 128 * (q + 1)]


def inverse(x):
    return pl.reciprocal(x, approx=True)


def kernel(
    sizes,
    slip,
    log_state,
    friction_a,
    friction_b,
    stress,
    leak,
    corner,
    fraction,
    row_basis,
    col_basis,
    far_row,
    far_col,
    far_rank,
    table,
    near_hbm,
    coupling_hbm,
    p_hbm,
    region_hbm,
    rate_hbm,
    accel_out,
    state_out,
    pv,
    rv,
    region,
    acc,
    snd,
    rcv,
    fsnd,
    frcv,
    p_edge,
    r_edge,
    wz,
    wyx,
    p_low,
    near,
    coupling,
    pick,
    gather_x,
    gather,
    slip_edge,
    window,
    flow_row,
    fp_row,
    fp_own,
    fp_other,
    near_own,
    near_other,
    tot_own,
    tot_other,
    block,
    far16,
    load_sem,
    x_send,
    x_recv,
    z_send,
    z_recv,
    y_send,
    y_recv,
    pr_send,
    pr_recv,
    fl_send,
    fl_recv,
    one_send,
    one_recv,
    out_sem,
):
    ny, nz, nx = sizes
    slabs = ny * nz * nx
    planes, width_y, width_z = region.shape
    half = width_y // 2
    rows = half // PARTS
    rank = col_basis.shape[0]
    cells = corner.shape[1]
    yi, zi, xi = (lax.axis_index(name) for name in SLAB)
    bi = lax.axis_index("blk")
    slab = (yi * nz + zi) * nx + xi

    def chip_of(index):
        return (
            lax.div(index, nz * nx),
            lax.rem(lax.div(index, nx), nz),
            lax.rem(index, nx),
            bi,
        )

    above = chip_of(lax.rem(slab + 1, slabs))
    below = chip_of(lax.rem(slab + slabs - 1, slabs))
    other = (yi, zi, xi, 1 - bi)
    x_peers = [(yi, zi, lax.rem(xi + d, nx), bi) for d in range(1, nx)]
    z_peers = [(yi, lax.rem(zi + d, nz), xi, bi) for d in range(1, nz)]
    y_peers = [(lax.rem(yi + d, ny), zi, xi, bi) for d in range(1, ny)]

    barrier = pltpu.get_barrier_semaphore()
    peers = [above, below, other] + x_peers + z_peers + y_peers
    for peer in peers:
        pl.semaphore_signal(barrier, inc=1, device_id=peer, device_id_type=MESH)

    def remote(src, dst, send, recv, device):
        return pltpu.make_async_remote_copy(
            src_ref=src,
            dst_ref=dst,
            send_sem=send,
            recv_sem=recv,
            device_id=device,
            device_id_type=MESH,
        )

    def quarter(plane, part, sem):
        at = pl.ds(part * half, half)
        to = pl.ds(HALO + part * half, half)
        return (
            pltpu.make_async_copy(
                region_hbm.at[plane, at], region.at[plane, at], load_sem.at[sem]
            ),
            pltpu.make_async_copy(p_hbm.at[plane, at], pv.at[plane, to], load_sem.at[sem + 1]),
        )

    first_up, first_down = quarter(1, 0, 0), quarter(0, 1, 2)
    later = quarter(0, 0, 4) + quarter(1, 1, 6)
    load_near = pltpu.make_async_copy(near_hbm, near, load_sem.at[8])
    load_coupling = pltpu.make_async_copy(coupling_hbm, coupling, load_sem.at[9])
    for copy in first_up + first_down + later + (load_near, load_coupling):
        copy.start()

    for c in range(4):
        window[1 + c : 2 + c, :] = lanes_row(slip, 4 * c, 4)
    slip_row = jnp.concatenate([window[1 + c : 2 + c, :] for c in range(4)], axis=1)
    spread = jnp.broadcast_to(slip_row, (8, cells))
    lane = lax.broadcasted_iota(jnp.int32, (8, cells), 1)
    sub = lax.broadcasted_iota(jnp.int32, (8, cells), 0)
    spread = jnp.where(
        (lane >= sub * 512) & (lane < sub * 512 + 512), spread, jnp.float32(0.0)
    ).astype(jnp.bfloat16)
    moments = lax.dot_general(
        spread, col_basis[...], (((1,), (1,)), ((), ())), preferred_element_type=jnp.float32
    )
    gather_x[xi] = jnp.zeros((8, 128), jnp.float32)
    gather_x[xi, :, 0:rank] = moments
    for c in range(16):
        flow_row[:, 128 * c : 128 * (c + 1)] = leak[c : c + 1, :] * slip[c : c + 1, :]

    pl.semaphore_wait(barrier, len(peers))

    x_copies = [
        remote(gather_x.at[xi], gather_x.at[xi], x_send.at[d], x_recv.at[d], peer)
        for d, peer in enumerate(x_peers)
    ]
    for copy in x_copies:
        copy.start()
    slip_up = remote(slip.at[8:16], slip_edge.at[0], one_send.at[0], one_recv.at[0], above)
    slip_down = remote(slip.at[0:8], slip_edge.at[1], one_send.at[1], one_recv.at[1], below)
    slip_up.start()
    slip_down.start()

    def look_up(plane, start, count):
        chosen = region[plane, pl.ds(start, count), :]
        entries = jnp.broadcast_to(table[0:1, :], (count, 128))
        r = jnp.concatenate(
            [
                jnp.take_along_axis(
                    entries,
                    chosen[:, 128 * j : 128 * (j + 1)],
                    axis=1,
                    mode="promise_in_bounds",
                )
                for j in range(width_z // 128)
            ],
            axis=1,
        )
        p = pv[plane, pl.ds(HALO + start, count), :].astype(jnp.bfloat16)
        rv[plane, pl.ds(HALO + start, count), :] = r
        p_low[pl.ds(plane * width_y + start, count), :] = p
        return p, r.astype(jnp.bfloat16)

    pr_copies = []
    for part in range(PARTS):
        for way, plane, offset, device, loads in (
            (0, 1, 0, above, first_up),
            (1, 0, half, below, first_down),
        ):
            if part == 0:
                for copy in loads:
                    copy.wait()
            p, r = look_up(plane, offset + part * rows, rows)
            snd[way, part, 0] = p
            snd[way, part, 1] = r
            copy = remote(
                snd.at[way, part],
                rcv.at[way, part],
                pr_send.at[way, part],
                pr_recv.at[way, part],
                device,
            )
            copy.start()
            pr_copies.append(copy)

    for copy in later:
        copy.wait()

    def rest(step, carry):
        start = pl.multiple_of(step * rows, rows)
        look_up(0, start, rows)
        look_up(1, start + half, rows)
        return carry

    lax.fori_loop(0, PARTS, rest, 0)

    edge = pl.multiple_of(HALO + (1 - bi) * (width_y - 8), 8)
    p_copy = remote(
        pv.at[:, pl.ds(edge, 8), :], p_edge, one_send.at[2], one_recv.at[2], other
    )
    r_copy = remote(
        rv.at[:, pl.ds(edge, 8), :], r_edge, one_send.at[3], one_recv.at[3], other
    )
    p_copy.start()
    r_copy.start()

    for copy in x_copies:
        copy.wait_recv()
    mine = jnp.concatenate([gather_x[i, 0:4, :] for i in range(nx)], axis=0)
    gather[yi, zi] = mine.astype(jnp.bfloat16)
    z_copies = [
        remote(gather.at[yi, zi], gather.at[yi, zi], z_send.at[d], z_recv.at[d], peer)
        for d, peer in enumerate(z_peers)
    ]
    for copy in z_copies:
        copy.start()

    y_start = bi * width_y

    def sample(step, carry):
        at = pl.ds(pl.multiple_of(step * F_TILE, F_TILE), F_TILE)
        z = corner[2:3, at]
        fz = fraction[2:3, at]
        iota = lax.broadcasted_iota(jnp.int32, (width_z, F_TILE), 0)
        weight = jnp.where(
            iota == z, 1.0 - fz, jnp.where(iota == z + 1, fz, jnp.float32(0.0))
        ).astype(jnp.bfloat16)
        wz[:, at] = weight
        along_z = jnp.dot(p_low[...], weight, preferred_element_type=jnp.float32)
        y = corner[1:2, at] - y_start
        fy = fraction[1:2, at]
        fx = fraction[0:1, at]
        flow = flow_row[:, at]
        iota = lax.broadcasted_iota(jnp.int32, (width_y, F_TILE), 0)
        weight_y = jnp.where(iota == y, 1.0 - fy, jnp.where(iota == y + 1, fy, jnp.float32(0.0)))
        low = jnp.sum(along_z[:width_y] * weight_y, axis=0, keepdims=True)
        high = jnp.sum(along_z[width_y:] * weight_y, axis=0, keepdims=True)
        fp_row[:, at] = (1.0 - fx) * low + fx * high
        wyx[0:width_y, at] = (weight_y * ((1.0 - fx) * flow)).astype(jnp.bfloat16)
        wyx[width_y:, at] = (weight_y * (fx * flow)).astype(jnp.bfloat16)
        return carry

    steps = cells // F_TILE
    lax.fori_loop(0, steps // 2, sample, 0)

    for copy in z_copies:
        copy.wait_recv()
    y_copies = [
        remote(gather.at[yi], gather.at[yi], y_send.at[d], y_recv.at[d], peer)
        for d, peer in enumerate(y_peers)
    ]
    for copy in y_copies:
        copy.start()

    has_below = jnp.where(slab > 0, 1.0, 0.0).astype(jnp.float32)
    has_above = jnp.where(slab < slabs - 1, 1.0, 0.0).astype(jnp.float32)
    fl_copies = {}

    def faces(part):
        for way, plane, offset, device, present in (
            (0, 0, 0, below, has_below),
            (1, 1, half, above, has_above),
        ):
            pr_copies[2 * part + way].wait_recv()
            at = pl.ds(HALO + offset + part * rows, rows)
            p_in = rcv[way, part, 0].astype(jnp.float32)
            r_in = rcv[way, part, 1].astype(jnp.float32)
            drop = pv[plane, at, :] - p_in
            flux = drop * (inverse(rv[plane, at, :] + r_in) * -present)
            fsnd[way, part] = flux.astype(jnp.bfloat16)
            copy = remote(
                fsnd.at[way, part],
                frcv.at[way, part],
                fl_send.at[way, part],
                fl_recv.at[way, part],
                device,
            )
            copy.start()
            fl_copies[way, part] = copy

    faces(0)
    lax.fori_loop(steps // 2, steps, sample, 0)
    for c in range(16):
        fp_own[c : c + 1, :] = fp_row[:, 128 * c : 128 * (c + 1)]
    fp_copy = remote(fp_own, fp_other, one_send.at[4], one_recv.at[4], other)
    fp_copy.start()
    faces(1)

    slip_up.wait_recv()
    slip_down.wait_recv()
    window[0:1, :] = has_below * jnp.concatenate(
        [slip_edge[0, 4 + q : 5 + q, :] for q in range(4)], axis=1
    )
    window[5:6, :] = has_above * jnp.concatenate(
        [slip_edge[1, q : 1 + q, :] for q in range(4)], axis=1
    )
    load_near.wait()
    for i in range(2):
        total = jnp.zeros((8, 512), jnp.float32)
        for j in range(3):
            row = window[pl.ds(2 * bi + i + j, 1), :]
            row = jnp.broadcast_to(row, (8, 512)).astype(jnp.bfloat16)
            total = total + lax.dot_general(
                row, near[i, j], (((1,), (1,)), ((), ())), preferred_element_type=jnp.float32
            )
        store_rows(near_own, 4 * i, total[0:1, :])
    near_copy = remote(near_own, near_other, one_send.at[5], one_recv.at[5], other)
    near_copy.start()

    column = lanes_row(far_col, 0, 8)
    pick[...] = jnp.where(
        lax.broadcasted_iota(jnp.int32, pick.shape, 0) == column, 1.0, 0.0
    ).astype(jnp.bfloat16)
    for copy in y_copies:
        copy.wait_recv()
    moments = gather[...].reshape(512, 128)[:, 0:rank]
    picked = lax.dot_general(
        moments, pick[...], (((0,), (0,)), ((), ())), preferred_element_type=jnp.float32
    )
    ranks = lanes_row(far_rank, 0, 8)
    masked = jnp.where(
        lax.broadcasted_iota(jnp.int32, picked.shape, 0) < ranks, picked, jnp.float32(0.0)
    )
    load_coupling.wait()
    for a in range(rank):
        block[a : a + 1, :] = jnp.sum(
            coupling[a].astype(jnp.float32) * masked, axis=0, keepdims=True
        )
    target = lanes_row(far_row, 0, 8)
    lane = lax.broadcasted_iota(jnp.int32, (rank, 128), 1)
    totals = jnp.zeros((rank, 128), jnp.float32)
    for c in range(4):
        share = jnp.sum(
            jnp.where(target == c, block[...], jnp.float32(0.0)), axis=1, keepdims=True
        )
        totals = totals + jnp.where(lane == c, share, jnp.float32(0.0))
    tot_own[...] = totals
    tot_copy = remote(tot_own, tot_other, one_send.at[6], one_recv.at[6], other)
    tot_copy.start()

    def spread_source(step, carry):
        at = pl.ds(pl.multiple_of(step * 256, 256), 256)
        result = lax.dot_general(
            wyx[...], wz[at, :], (((1,), (1,)), ((), ())), preferred_element_type=jnp.float32
        )
        acc[0, :, at] = result[:width_y]
        acc[1, :, at] = result[width_y:]
        return carry

    lax.fori_loop(0, width_z // 256, spread_source, 0)
    faces(2)

    p_copy.wait_recv()
    r_copy.wait_recv()
    inner = (1 - bi).astype(jnp.float32)
    for plane in range(planes):
        p_lower, r_lower = p_edge[plane, 7:8, :], r_edge[plane, 7:8, :]
        p_upper, r_upper = p_edge[plane, 0:1, :], r_edge[plane, 0:1, :]
        pv[plane, 7:8, :] = p_lower
        rv[plane, 7:8, :] = r_lower + inner * FAR
        pv[plane, HALO + width_y : HALO + width_y + 1, :] = p_upper
        rv[plane, HALO + width_y : HALO + width_y + 1, :] = r_upper + (1.0 - inner) * FAR

    def stencil(step, carry):
        y = pl.multiple_of(step * 8, 8)
        p = [pv[plane, pl.ds(HALO + y, 8), :] for plane in range(planes)]
        r = [rv[plane, pl.ds(HALO + y, 8), :] for plane in range(planes)]
        last = lax.broadcasted_iota(jnp.int32, (8, width_z), 1) == width_z - 1
        between = (p[1] - p[0]) * inverse(r[0] + r[1])
        for plane in range(planes):
            pc, rc = p[plane], r[plane]
            total = acc[plane, pl.ds(y, 8), :]
            total = total + between if plane == 0 else total - between
            for shift in (1, -1):
                pn = pv.at[plane, pl.ds(y, 24), :][HALO + shift : HALO + shift + 8, :]
                rn = rv.at[plane, pl.ds(y, 24), :][HALO + shift : HALO + shift + 8, :]
                total = total + (pn - pc) * inverse(rn + rc)
            pn = pltpu.roll(pc, width_z - 1, 1)
            rn = pltpu.roll(rc, width_z - 1, 1)
            flux = jnp.where(last, jnp.float32(0.0), (pn - pc) * inverse(rn + rc))
            total = total + flux - pltpu.roll(flux, 1, 1)
            acc[plane, pl.ds(y, 8), :] = total
        return carry

    lax.fori_loop(0, width_y // 8, stencil, 0)
    faces(3)

    tot_copy.wait_recv()
    near_copy.wait_recv()
    fp_copy.wait_recv()
    totals = tot_own[...] + tot_other[...]
    for c in range(4):
        basis = row_basis[:, 512 * c : 512 * (c + 1)].astype(jnp.float32)
        store_rows(
            far16, 4 * c, jnp.sum(basis * totals[:, c : c + 1], axis=0, keepdims=True)
        )
    own, others = near_own[...], near_other[...]
    first = bi == 0
    near16 = jnp.concatenate(
        [jnp.where(first, own, others), jnp.where(first, others, own)], axis=0
    )
    traction = near16 + far16[...]
    effective = stress[...] - (fp_own[...] + fp_other[...])
    rate = slip[...]
    state_rate = jnp.exp(-log_state[...]) - rate
    accel_out[...] = (traction - effective * friction_b[...] * state_rate) / (
        effective * friction_a[...] / rate + 0.5
    )
    state_out[...] = state_rate

    stores = []
    for part in range(PARTS):
        low = pl.ds(part * rows, rows)
        high = pl.ds(half + part * rows, rows)
        for which, plane, at, flux in (
            (0, 0, low, fsnd.at[0, part]),
            (1, 1, high, fsnd.at[1, part]),
        ):
            value = flux[...].astype(jnp.float32)
            acc[plane, at, :] = acc[plane, at, :] + value
            copy = pltpu.make_async_copy(
                acc.at[plane, at], rate_hbm.at[plane, at], out_sem.at[which, part]
            )
            copy.start()
            stores.append(copy)
    for part in range(PARTS):
        low = pl.ds(part * rows, rows)
        high = pl.ds(half + part * rows, rows)
        for which, plane, at, way in ((2, 1, low, 0), (3, 0, high, 1)):
            fl_copies[way, part].wait_recv()
            value = frcv[way, part].astype(jnp.float32)
            acc[plane, at, :] = acc[plane, at, :] - value
            copy = pltpu.make_async_copy(
                acc.at[plane, at], rate_hbm.at[plane, at], out_sem.at[which, part]
            )
            copy.start()
            stores.append(copy)
    for copy in stores:
        copy.wait()
    sent = x_copies + z_copies + y_copies + pr_copies + list(fl_copies.values())
    for copy in sent + [slip_up, slip_down, p_copy, r_copy, fp_copy, near_copy, tot_copy]:
        copy.wait_send()


def shards(
    slip_rate,
    log_state,
    friction_a,
    friction_b,
    normal_stress,
    leak_rate,
    corner,
    fraction,
    near_blocks,
    row_basis,
    col_basis,
    far_row,
    far_col,
    far_rank,
    far_coupling,
    pressure,
    region,
    perm_table,
):
    sizes = tuple(lax.axis_size(name) for name in SLAB)
    ny, nz, nx = sizes
    planes, width_y, width_z = pressure.shape
    cells = slip_rate.shape[0]
    clusters = cells // 512
    slots = far_row.shape[0]
    rank = col_basis.shape[0]
    rows = width_y // 2 // PARTS
    f32, bf16 = jnp.float32, jnp.bfloat16
    table = jnp.broadcast_to(
        jnp.pad(0.5 / perm_table, (0, 128 - perm_table.shape[0])), (8, 128)
    )
    vmem = pl.BlockSpec(memory_space=pltpu.VMEM)
    hbm = pl.BlockSpec(memory_space=pl.ANY)
    dma = pltpu.SemaphoreType.DMA

    def cut(x):
        return x.reshape(-1, 128)

    rate, accel, state = pl.pallas_call(
        functools.partial(kernel, sizes),
        out_shape=(
            jax.ShapeDtypeStruct(pressure.shape, f32),
            jax.ShapeDtypeStruct((cells // 128, 128), f32),
            jax.ShapeDtypeStruct((cells // 128, 128), f32),
        ),
        in_specs=[vmem] * 14 + [hbm] * 4,
        out_specs=(hbm, vmem, vmem),
        scratch_shapes=[
            pltpu.VMEM((planes, width_y + 2 * HALO, width_z), f32),
            pltpu.VMEM((planes, width_y + 2 * HALO, width_z), f32),
            pltpu.VMEM((planes, width_y, width_z), jnp.int32),
            pltpu.VMEM((planes, width_y, width_z), f32),
            pltpu.VMEM((2, PARTS, 2, rows, width_z), bf16),
            pltpu.VMEM((2, PARTS, 2, rows, width_z), bf16),
            pltpu.VMEM((2, PARTS, rows, width_z), bf16),
            pltpu.VMEM((2, PARTS, rows, width_z), bf16),
            pltpu.VMEM((planes, 8, width_z), f32),
            pltpu.VMEM((planes, 8, width_z), f32),
            pltpu.VMEM((width_z, cells), bf16),
            pltpu.VMEM((planes * width_y, cells), bf16),
            pltpu.VMEM((planes * width_y, width_z), bf16),
            pltpu.VMEM(near_blocks.shape, bf16),
            pltpu.VMEM(far_coupling.shape, bf16),
            pltpu.VMEM((ny * nz * nx * clusters, slots), bf16),
            pltpu.VMEM((nx, 8, 128), f32),
            pltpu.VMEM((ny, nz, nx * clusters, 128), bf16),
            pltpu.VMEM((2, 8, 128), f32),
            pltpu.VMEM((8, 512), f32),
            pltpu.VMEM((1, cells), f32),
            pltpu.VMEM((1, cells), f32),
            pltpu.VMEM((cells // 128, 128), f32),
            pltpu.VMEM((cells // 128, 128), f32),
            pltpu.VMEM((8, 128), f32),
            pltpu.VMEM((8, 128), f32),
            pltpu.VMEM((rank, 128), f32),
            pltpu.VMEM((rank, 128), f32),
            pltpu.VMEM((rank, slots), f32),
            pltpu.VMEM((cells // 128, 128), f32),
            dma((10,)),
            dma((nx - 1,)),
            dma((nx - 1,)),
            dma((nz - 1,)),
            dma((nz - 1,)),
            dma((ny - 1,)),
            dma((ny - 1,)),
            dma((2, PARTS)),
            dma((2, PARTS)),
            dma((2, PARTS)),
            dma((2, PARTS)),
            dma((7,)),
            dma((7,)),
            dma((4, PARTS)),
        ],
        compiler_params=pltpu.CompilerParams(
            collective_id=0, has_side_effects=True, vmem_limit_bytes=48 * 1024 * 1024
        ),
        name="fault_step",
    )(
        cut(slip_rate),
        cut(log_state),
        cut(friction_a),
        cut(friction_b),
        cut(normal_stress),
        cut(leak_rate),
        corner,
        fraction,
        row_basis,
        col_basis,
        cut(far_row),
        cut(far_col),
        cut(far_rank),
        table,
        near_blocks,
        far_coupling,
        pressure,
        region,
    )
    return accel.reshape(cells), state.reshape(cells), rate


def solution(mesh):
    torus = Mesh(
        mesh.devices.reshape(4, 8, 4, mesh.shape["blk"]), ("slab_0", "slab_1", "slab_2", "blk")
    )
    placed = (
        P(SLAB),
        P(SLAB),
        P(SLAB),
        P(SLAB),
        P(SLAB),
        P(SLAB),
        P(None, SLAB),
        P(None, SLAB),
        P(SLAB_BLK, None, None, None),
        P(None, SLAB),
        P(None, SLAB),
        P(SLAB_BLK),
        P(SLAB_BLK),
        P(SLAB_BLK),
        P(None, None, SLAB_BLK),
        P(SLAB, "blk", None),
        P(SLAB, "blk", None),
        P(),
    )
    return jax.shard_map(
        shards,
        mesh=torus,
        in_specs=placed,
        out_specs=(P(SLAB), P(SLAB), P(SLAB, "blk", None)),
        check_vma=False,
    )
```

```python
import functools

import jax
import jax.numpy as jnp
from jax import lax
from jax.experimental import pallas as pl
from jax.experimental.pallas import tpu as pltpu
from jax.sharding import Mesh
from jax.sharding import PartitionSpec as P

SLAB = ("slab_0", "slab_1", "slab_2")
SLAB_BLK = ("slab_0", "slab_1", "slab_2", "blk")
MESH = pl.DeviceIdType.MESH

PARTS = 4
F_TILE = 256
HALO = 8
FAR = 1e30


def lanes_row(ref, first, count):
    return jnp.concatenate([ref[first + q : first + q + 1, :] for q in range(count)], axis=1)


def store_rows(ref, first, row):
    for q in range(row.shape[1] // 128):
        ref[first + q : first + q + 1, :] = row[:, 128 * q : 128 * (q + 1)]


def inverse(x):
    return pl.reciprocal(x, approx=True)


def kernel(
    sizes,
    slip_hbm,
    log_state_hbm,
    friction_a_hbm,
    friction_b_hbm,
    stress_hbm,
    leak_hbm,
    corner_hbm,
    fraction_hbm,
    row_basis_hbm,
    col_basis_hbm,
    far_row_hbm,
    far_col_hbm,
    far_rank_hbm,
    table_hbm,
    near_hbm,
    coupling_hbm,
    p_hbm,
    region_hbm,
    rate_hbm,
    accel_out,
    state_out,
    slip,
    log_state,
    friction_a,
    friction_b,
    stress,
    leak,
    corner,
    fraction,
    row_basis,
    col_basis,
    far_row,
    far_col,
    far_rank,
    table,
    pv,
    rv,
    region,
    acc,
    snd,
    rcv,
    fsnd,
    frcv,
    p_edge,
    r_edge,
    wz,
    wyx,
    p_low,
    near,
    coupling,
    pick,
    gather_x,
    gather,
    slip_edge,
    window,
    flow_row,
    fp_row,
    fp_own,
    fp_other,
    near_own,
    near_other,
    tot_own,
    tot_other,
    block,
    far16,
    load_sem,
    x_send,
    x_recv,
    z_send,
    z_recv,
    y_send,
    y_recv,
    pr_send,
    pr_recv,
    fl_send,
    fl_recv,
    one_send,
    one_recv,
    out_sem,
):
    ny, nz, nx = sizes
    slabs = ny * nz * nx
    planes, width_y, width_z = region.shape
    half = width_y // 2
    rows = half // PARTS
    rank = col_basis.shape[0]
    cells = corner.shape[1]
    yi, zi, xi = (lax.axis_index(name) for name in SLAB)
    bi = lax.axis_index("blk")
    slab = (yi * nz + zi) * nx + xi

    def chip_of(index):
        return (
            lax.div(index, nz * nx),
            lax.rem(lax.div(index, nx), nz),
            lax.rem(index, nx),
            bi,
        )

    above = chip_of(lax.rem(slab + 1, slabs))
    below = chip_of(lax.rem(slab + slabs - 1, slabs))
    other = (yi, zi, xi, 1 - bi)
    x_peers = [(yi, zi, lax.rem(xi + d, nx), bi) for d in range(1, nx)]
    z_peers = [(yi, lax.rem(zi + d, nz), xi, bi) for d in range(1, nz)]
    y_peers = [(lax.rem(yi + d, ny), zi, xi, bi) for d in range(1, ny)]

    barrier = pltpu.get_barrier_semaphore()
    peers = [above, below, other] + x_peers + z_peers + y_peers
    for peer in peers:
        pl.semaphore_signal(barrier, inc=1, device_id=peer, device_id_type=MESH)

    def remote(src, dst, send, recv, device):
        return pltpu.make_async_remote_copy(
            src_ref=src,
            dst_ref=dst,
            send_sem=send,
            recv_sem=recv,
            device_id=device,
            device_id_type=MESH,
        )

    def quarter(plane, part, sem):
        at = pl.ds(part * half, half)
        to = pl.ds(HALO + part * half, half)
        return (
            pltpu.make_async_copy(
                region_hbm.at[plane, at], region.at[plane, at], load_sem.at[sem]
            ),
            pltpu.make_async_copy(p_hbm.at[plane, at], pv.at[plane, to], load_sem.at[sem + 1]),
        )

    first_up, first_down = quarter(1, 0, 0), quarter(0, 1, 2)
    later = quarter(0, 0, 4) + quarter(1, 1, 6)
    small = [
        pltpu.make_async_copy(src, dst, load_sem.at[10 + i])
        for i, (src, dst) in enumerate(
            (
                (slip_hbm, slip),
                (col_basis_hbm, col_basis),
                (table_hbm, table),
                (leak_hbm, leak),
                (corner_hbm, corner),
                (fraction_hbm, fraction),
                (far_col_hbm, far_col),
                (far_rank_hbm, far_rank),
                (far_row_hbm, far_row),
                (row_basis_hbm, row_basis),
                (stress_hbm, stress),
                (log_state_hbm, log_state),
                (friction_a_hbm, friction_a),
                (friction_b_hbm, friction_b),
            )
        )
    ]
    load_near = pltpu.make_async_copy(near_hbm, near, load_sem.at[8])
    load_coupling = pltpu.make_async_copy(coupling_hbm, coupling, load_sem.at[9])
    ahead = small[:4]
    behind = small[4:6]
    last = small[6:]
    for copy in ahead[:3] + list(first_up + first_down) + ahead[3:] + behind + list(later):
        copy.start()
    for copy in [load_near, load_coupling] + last:
        copy.start()
    for copy in ahead:
        copy.wait()

    for c in range(4):
        window[1 + c : 2 + c, :] = lanes_row(slip, 4 * c, 4)
    slip_row = jnp.concatenate([window[1 + c : 2 + c, :] for c in range(4)], axis=1)
    spread = jnp.broadcast_to(slip_row, (8, cells))
    lane = lax.broadcasted_iota(jnp.int32, (8, cells), 1)
    sub = lax.broadcasted_iota(jnp.int32, (8, cells), 0)
    spread = jnp.where(
        (lane >= sub * 512) & (lane < sub * 512 + 512), spread, jnp.float32(0.0)
    ).astype(jnp.bfloat16)
    moments = lax.dot_general(
        spread, col_basis[...], (((1,), (1,)), ((), ())), preferred_element_type=jnp.float32
    )
    gather_x[xi] = jnp.zeros((8, 128), jnp.float32)
    gather_x[xi, :, 0:rank] = moments
    for c in range(16):
        flow_row[:, 128 * c : 128 * (c + 1)] = leak[c : c + 1, :] * slip[c : c + 1, :]

    pl.semaphore_wait(barrier, len(peers))

    x_copies = [
        remote(gather_x.at[xi], gather_x.at[xi], x_send.at[d], x_recv.at[d], peer)
        for d, peer in enumerate(x_peers)
    ]
    for copy in x_copies:
        copy.start()
    slip_up = remote(slip.at[8:16], slip_edge.at[0], one_send.at[0], one_recv.at[0], above)
    slip_down = remote(slip.at[0:8], slip_edge.at[1], one_send.at[1], one_recv.at[1], below)
    slip_up.start()
    slip_down.start()

    halves = jnp.concatenate([0.5 / table[...], jnp.zeros((1, 128 - table.shape[1]), jnp.float32)], axis=1)

    def look_up(plane, start, count):
        chosen = region[plane, pl.ds(start, count), :]
        entries = jnp.broadcast_to(halves, (count, 128))
        r = jnp.concatenate(
            [
                jnp.take_along_axis(
                    entries,
                    chosen[:, 128 * j : 128 * (j + 1)],
                    axis=1,
                    mode="promise_in_bounds",
                )
                for j in range(width_z // 128)
            ],
            axis=1,
        )
        p = pv[plane, pl.ds(HALO + start, count), :].astype(jnp.bfloat16)
        rv[plane, pl.ds(HALO + start, count), :] = r
        p_low[pl.ds(plane * width_y + start, count), :] = p
        return p, r.astype(jnp.bfloat16)

    pr_copies = []
    for part in range(PARTS):
        for way, plane, offset, device, loads in (
            (0, 1, 0, above, first_up),
            (1, 0, half, below, first_down),
        ):
            if part == 0:
                for copy in loads:
                    copy.wait()
            p, r = look_up(plane, offset + part * rows, rows)
            snd[way, part, 0] = p
            snd[way, part, 1] = r
            copy = remote(
                snd.at[way, part],
                rcv.at[way, part],
                pr_send.at[way, part],
                pr_recv.at[way, part],
                device,
            )
            copy.start()
            pr_copies.append(copy)

    for copy in later + tuple(behind):
        copy.wait()

    def rest(step, carry):
        start = pl.multiple_of(step * rows, rows)
        look_up(0, start, rows)
        look_up(1, start + half, rows)
        return carry

    lax.fori_loop(0, PARTS, rest, 0)

    edge = pl.multiple_of(HALO + (1 - bi) * (width_y - 8), 8)
    p_copy = remote(
        pv.at[:, pl.ds(edge, 8), :], p_edge, one_send.at[2], one_recv.at[2], other
    )
    r_copy = remote(
        rv.at[:, pl.ds(edge, 8), :], r_edge, one_send.at[3], one_recv.at[3], other
    )
    p_copy.start()
    r_copy.start()

    for copy in x_copies:
        copy.wait_recv()
    mine = jnp.concatenate([gather_x[i, 0:4, :] for i in range(nx)], axis=0)
    gather[yi, zi] = mine.astype(jnp.bfloat16)
    z_copies = [
        remote(gather.at[yi, zi], gather.at[yi, zi], z_send.at[d], z_recv.at[d], peer)
        for d, peer in enumerate(z_peers)
    ]
    for copy in z_copies:
        copy.start()

    y_start = bi * width_y

    def sample(step, carry):
        at = pl.ds(pl.multiple_of(step * F_TILE, F_TILE), F_TILE)
        z = corner[2:3, at]
        fz = fraction[2:3, at]
        iota = lax.broadcasted_iota(jnp.int32, (width_z, F_TILE), 0)
        weight = jnp.where(
            iota == z, 1.0 - fz, jnp.where(iota == z + 1, fz, jnp.float32(0.0))
        ).astype(jnp.bfloat16)
        wz[:, at] = weight
        along_z = jnp.dot(p_low[...], weight, preferred_element_type=jnp.float32)
        y = corner[1:2, at] - y_start
        fy = fraction[1:2, at]
        fx = fraction[0:1, at]
        flow = flow_row[:, at]
        iota = lax.broadcasted_iota(jnp.int32, (width_y, F_TILE), 0)
        weight_y = jnp.where(iota == y, 1.0 - fy, jnp.where(iota == y + 1, fy, jnp.float32(0.0)))
        low = jnp.sum(along_z[:width_y] * weight_y, axis=0, keepdims=True)
        high = jnp.sum(along_z[width_y:] * weight_y, axis=0, keepdims=True)
        fp_row[:, at] = (1.0 - fx) * low + fx * high
        wyx[0:width_y, at] = (weight_y * ((1.0 - fx) * flow)).astype(jnp.bfloat16)
        wyx[width_y:, at] = (weight_y * (fx * flow)).astype(jnp.bfloat16)
        return carry

    steps = cells // F_TILE
    lax.fori_loop(0, steps // 2, sample, 0)

    for copy in z_copies:
        copy.wait_recv()
    y_copies = [
        remote(gather.at[yi], gather.at[yi], y_send.at[d], y_recv.at[d], peer)
        for d, peer in enumerate(y_peers)
    ]
    for copy in y_copies:
        copy.start()

    has_below = jnp.where(slab > 0, 1.0, 0.0).astype(jnp.float32)
    has_above = jnp.where(slab < slabs - 1, 1.0, 0.0).astype(jnp.float32)
    fl_copies = {}

    def faces(part):
        for way, plane, offset, device, present in (
            (0, 0, 0, below, has_below),
            (1, 1, half, above, has_above),
        ):
            pr_copies[2 * part + way].wait_recv()
            at = pl.ds(HALO + offset + part * rows, rows)
            p_in = rcv[way, part, 0].astype(jnp.float32)
            r_in = rcv[way, part, 1].astype(jnp.float32)
            drop = pv[plane, at, :] - p_in
            flux = drop * (inverse(rv[plane, at, :] + r_in) * -present)
            fsnd[way, part] = flux.astype(jnp.bfloat16)
            copy = remote(
                fsnd.at[way, part],
                frcv.at[way, part],
                fl_send.at[way, part],
                fl_recv.at[way, part],
                device,
            )
            copy.start()
            fl_copies[way, part] = copy

    faces(0)
    lax.fori_loop(steps // 2, steps, sample, 0)
    for c in range(16):
        fp_own[c : c + 1, :] = fp_row[:, 128 * c : 128 * (c + 1)]
    fp_copy = remote(fp_own, fp_other, one_send.at[4], one_recv.at[4], other)
    fp_copy.start()
    faces(1)

    slip_up.wait_recv()
    slip_down.wait_recv()
    window[0:1, :] = has_below * jnp.concatenate(
        [slip_edge[0, 4 + q : 5 + q, :] for q in range(4)], axis=1
    )
    window[5:6, :] = has_above * jnp.concatenate(
        [slip_edge[1, q : 1 + q, :] for q in range(4)], axis=1
    )
    load_near.wait()
    for i in range(2):
        total = jnp.zeros((8, 512), jnp.float32)
        for j in range(3):
            row = window[pl.ds(2 * bi + i + j, 1), :]
            row = jnp.broadcast_to(row, (8, 512)).astype(jnp.bfloat16)
            total = total + lax.dot_general(
                row, near[i, j], (((1,), (1,)), ((), ())), preferred_element_type=jnp.float32
            )
        store_rows(near_own, 4 * i, total[0:1, :])
    near_copy = remote(near_own, near_other, one_send.at[5], one_recv.at[5], other)
    near_copy.start()

    for copy in last:
        copy.wait()
    column = lanes_row(far_col, 0, 8)
    pick[...] = jnp.where(
        lax.broadcasted_iota(jnp.int32, pick.shape, 0) == column, 1.0, 0.0
    ).astype(jnp.bfloat16)
    for copy in y_copies:
        copy.wait_recv()
    moments = gather[...].reshape(512, 128)[:, 0:rank]
    picked = lax.dot_general(
        moments, pick[...], (((0,), (0,)), ((), ())), preferred_element_type=jnp.float32
    )
    ranks = lanes_row(far_rank, 0, 8)
    masked = jnp.where(
        lax.broadcasted_iota(jnp.int32, picked.shape, 0) < ranks, picked, jnp.float32(0.0)
    )
    load_coupling.wait()
    for a in range(rank):
        block[a : a + 1, :] = jnp.sum(
            coupling[a].astype(jnp.float32) * masked, axis=0, keepdims=True
        )
    target = lanes_row(far_row, 0, 8)
    lane = lax.broadcasted_iota(jnp.int32, (rank, 128), 1)
    totals = jnp.zeros((rank, 128), jnp.float32)
    for c in range(4):
        share = jnp.sum(
            jnp.where(target == c, block[...], jnp.float32(0.0)), axis=1, keepdims=True
        )
        totals = totals + jnp.where(lane == c, share, jnp.float32(0.0))
    tot_own[...] = totals
    tot_copy = remote(tot_own, tot_other, one_send.at[6], one_recv.at[6], other)
    tot_copy.start()

    def spread_source(step, carry):
        at = pl.ds(pl.multiple_of(step * 256, 256), 256)
        result = lax.dot_general(
            wyx[...], wz[at, :], (((1,), (1,)), ((), ())), preferred_element_type=jnp.float32
        )
        acc[0, :, at] = result[:width_y]
        acc[1, :, at] = result[width_y:]
        return carry

    lax.fori_loop(0, width_z // 256, spread_source, 0)
    faces(2)

    p_copy.wait_recv()
    r_copy.wait_recv()
    inner = (1 - bi).astype(jnp.float32)
    for plane in range(planes):
        p_lower, r_lower = p_edge[plane, 7:8, :], r_edge[plane, 7:8, :]
        p_upper, r_upper = p_edge[plane, 0:1, :], r_edge[plane, 0:1, :]
        pv[plane, 7:8, :] = p_lower
        rv[plane, 7:8, :] = r_lower + inner * FAR
        pv[plane, HALO + width_y : HALO + width_y + 1, :] = p_upper
        rv[plane, HALO + width_y : HALO + width_y + 1, :] = r_upper + (1.0 - inner) * FAR

    def stencil(step, carry):
        y = pl.multiple_of(step * 8, 8)
        p = [pv[plane, pl.ds(HALO + y, 8), :] for plane in range(planes)]
        r = [rv[plane, pl.ds(HALO + y, 8), :] for plane in range(planes)]
        last = lax.broadcasted_iota(jnp.int32, (8, width_z), 1) == width_z - 1
        between = (p[1] - p[0]) * inverse(r[0] + r[1])
        for plane in range(planes):
            pc, rc = p[plane], r[plane]
            total = acc[plane, pl.ds(y, 8), :]
            total = total + between if plane == 0 else total - between
            for shift in (1, -1):
                pn = pv.at[plane, pl.ds(y, 24), :][HALO + shift : HALO + shift + 8, :]
                rn = rv.at[plane, pl.ds(y, 24), :][HALO + shift : HALO + shift + 8, :]
                total = total + (pn - pc) * inverse(rn + rc)
            pn = pltpu.roll(pc, width_z - 1, 1)
            rn = pltpu.roll(rc, width_z - 1, 1)
            flux = jnp.where(last, jnp.float32(0.0), (pn - pc) * inverse(rn + rc))
            total = total + flux - pltpu.roll(flux, 1, 1)
            acc[plane, pl.ds(y, 8), :] = total
        return carry

    lax.fori_loop(0, width_y // 8, stencil, 0)
    faces(3)

    tot_copy.wait_recv()
    near_copy.wait_recv()
    fp_copy.wait_recv()
    totals = tot_own[...] + tot_other[...]
    for c in range(4):
        basis = row_basis[:, 512 * c : 512 * (c + 1)].astype(jnp.float32)
        store_rows(
            far16, 4 * c, jnp.sum(basis * totals[:, c : c + 1], axis=0, keepdims=True)
        )
    own, others = near_own[...], near_other[...]
    first = bi == 0
    near16 = jnp.concatenate(
        [jnp.where(first, own, others), jnp.where(first, others, own)], axis=0
    )
    traction = near16 + far16[...]
    effective = stress[...] - (fp_own[...] + fp_other[...])
    rate = slip[...]
    state_rate = jnp.exp(-log_state[...]) - rate
    accel_out[...] = (traction - effective * friction_b[...] * state_rate) / (
        effective * friction_a[...] / rate + 0.5
    )
    state_out[...] = state_rate

    stores = []
    for part in range(PARTS):
        low = pl.ds(part * rows, rows)
        high = pl.ds(half + part * rows, rows)
        for which, plane, at, flux in (
            (0, 0, low, fsnd.at[0, part]),
            (1, 1, high, fsnd.at[1, part]),
        ):
            value = flux[...].astype(jnp.float32)
            acc[plane, at, :] = acc[plane, at, :] + value
            copy = pltpu.make_async_copy(
                acc.at[plane, at], rate_hbm.at[plane, at], out_sem.at[which, part]
            )
            copy.start()
            stores.append(copy)
    for part in range(PARTS):
        low = pl.ds(part * rows, rows)
        high = pl.ds(half + part * rows, rows)
        for which, plane, at, way in ((2, 1, low, 0), (3, 0, high, 1)):
            fl_copies[way, part].wait_recv()
            value = frcv[way, part].astype(jnp.float32)
            acc[plane, at, :] = acc[plane, at, :] - value
            copy = pltpu.make_async_copy(
                acc.at[plane, at], rate_hbm.at[plane, at], out_sem.at[which, part]
            )
            copy.start()
            stores.append(copy)
    for copy in stores:
        copy.wait()
    sent = x_copies + z_copies + y_copies + pr_copies + list(fl_copies.values())
    for copy in sent + [slip_up, slip_down, p_copy, r_copy, fp_copy, near_copy, tot_copy]:
        copy.wait_send()


def shards(
    slip_rate,
    log_state,
    friction_a,
    friction_b,
    normal_stress,
    leak_rate,
    corner,
    fraction,
    near_blocks,
    row_basis,
    col_basis,
    far_row,
    far_col,
    far_rank,
    far_coupling,
    pressure,
    region,
    perm_table,
):
    sizes = tuple(lax.axis_size(name) for name in SLAB)
    ny, nz, nx = sizes
    planes, width_y, width_z = pressure.shape
    cells = slip_rate.shape[0]
    clusters = cells // 512
    slots = far_row.shape[0]
    rank = col_basis.shape[0]
    rows = width_y // 2 // PARTS
    f32, bf16 = jnp.float32, jnp.bfloat16
    vmem = pl.BlockSpec(memory_space=pltpu.VMEM)
    hbm = pl.BlockSpec(memory_space=pl.ANY)
    dma = pltpu.SemaphoreType.DMA

    def cut(x):
        return x.reshape(-1, 128)

    rate, accel, state = pl.pallas_call(
        functools.partial(kernel, sizes),
        out_shape=(
            jax.ShapeDtypeStruct(pressure.shape, f32),
            jax.ShapeDtypeStruct((cells // 128, 128), f32),
            jax.ShapeDtypeStruct((cells // 128, 128), f32),
        ),
        in_specs=[hbm] * 18,
        out_specs=(hbm, vmem, vmem),
        scratch_shapes=[
            *[pltpu.VMEM((cells // 128, 128), f32)] * 6,
            pltpu.VMEM(corner.shape, jnp.int32),
            pltpu.VMEM(fraction.shape, f32),
            pltpu.VMEM(row_basis.shape, bf16),
            pltpu.VMEM(col_basis.shape, bf16),
            *[pltpu.VMEM((slots // 128, 128), jnp.int32)] * 3,
            pltpu.VMEM((1, perm_table.shape[0]), f32),
            pltpu.VMEM((planes, width_y + 2 * HALO, width_z), f32),
            pltpu.VMEM((planes, width_y + 2 * HALO, width_z), f32),
            pltpu.VMEM((planes, width_y, width_z), jnp.int32),
            pltpu.VMEM((planes, width_y, width_z), f32),
            pltpu.VMEM((2, PARTS, 2, rows, width_z), bf16),
            pltpu.VMEM((2, PARTS, 2, rows, width_z), bf16),
            pltpu.VMEM((2, PARTS, rows, width_z), bf16),
            pltpu.VMEM((2, PARTS, rows, width_z), bf16),
            pltpu.VMEM((planes, 8, width_z), f32),
            pltpu.VMEM((planes, 8, width_z), f32),
            pltpu.VMEM((width_z, cells), bf16),
            pltpu.VMEM((planes * width_y, cells), bf16),
            pltpu.VMEM((planes * width_y, width_z), bf16),
            pltpu.VMEM(near_blocks.shape, bf16),
            pltpu.VMEM(far_coupling.shape, bf16),
            pltpu.VMEM((ny * nz * nx * clusters, slots), bf16),
            pltpu.VMEM((nx, 8, 128), f32),
            pltpu.VMEM((ny, nz, nx * clusters, 128), bf16),
            pltpu.VMEM((2, 8, 128), f32),
            pltpu.VMEM((8, 512), f32),
            pltpu.VMEM((1, cells), f32),
            pltpu.VMEM((1, cells), f32),
            pltpu.VMEM((cells // 128, 128), f32),
            pltpu.VMEM((cells // 128, 128), f32),
            pltpu.VMEM((8, 128), f32),
            pltpu.VMEM((8, 128), f32),
            pltpu.VMEM((rank, 128), f32),
            pltpu.VMEM((rank, 128), f32),
            pltpu.VMEM((rank, slots), f32),
            pltpu.VMEM((cells // 128, 128), f32),
            dma((24,)),
            dma((nx - 1,)),
            dma((nx - 1,)),
            dma((nz - 1,)),
            dma((nz - 1,)),
            dma((ny - 1,)),
            dma((ny - 1,)),
            dma((2, PARTS)),
            dma((2, PARTS)),
            dma((2, PARTS)),
            dma((2, PARTS)),
            dma((7,)),
            dma((7,)),
            dma((4, PARTS)),
        ],
        compiler_params=pltpu.CompilerParams(
            collective_id=0, has_side_effects=True, vmem_limit_bytes=60 * 1024 * 1024
        ),
        name="fault_step",
    )(
        cut(slip_rate),
        cut(log_state),
        cut(friction_a),
        cut(friction_b),
        cut(normal_stress),
        cut(leak_rate),
        corner,
        fraction,
        row_basis,
        col_basis,
        cut(far_row),
        cut(far_col),
        cut(far_rank),
        perm_table.reshape(1, -1),
        near_blocks,
        far_coupling,
        pressure,
        region,
    )
    return accel.reshape(cells), state.reshape(cells), rate


def solution(mesh):
    torus = Mesh(
        mesh.devices.reshape(4, 8, 4, mesh.shape["blk"]), ("slab_0", "slab_1", "slab_2", "blk")
    )
    placed = (
        P(SLAB),
        P(SLAB),
        P(SLAB),
        P(SLAB),
        P(SLAB),
        P(SLAB),
        P(None, SLAB),
        P(None, SLAB),
        P(SLAB_BLK, None, None, None),
        P(None, SLAB),
        P(None, SLAB),
        P(SLAB_BLK),
        P(SLAB_BLK),
        P(SLAB_BLK),
        P(None, None, SLAB_BLK),
        P(SLAB, "blk", None),
        P(SLAB, "blk", None),
        P(),
    )
    return jax.shard_map(
        shards,
        mesh=torus,
        in_specs=placed,
        out_specs=(P(SLAB), P(SLAB), P(SLAB, "blk", None)),
        check_vma=False,
    )
```

```python
import functools

import jax
import jax.numpy as jnp
from jax import lax
from jax.experimental import pallas as pl
from jax.experimental.pallas import tpu as pltpu
from jax.sharding import Mesh
from jax.sharding import PartitionSpec as P

SLAB = ("slab_0", "slab_1", "slab_2")
SLAB_BLK = ("slab_0", "slab_1", "slab_2", "blk")
MESH = pl.DeviceIdType.MESH

PARTS = 4
F_TILE = 512
Z_TILE = 256
HALO = 8
FAR = 1e30


def lanes_row(ref, first, count):
    return jnp.concatenate([ref[first + q : first + q + 1, :] for q in range(count)], axis=1)


def store_rows(ref, first, row):
    for q in range(row.shape[1] // 128):
        ref[first + q : first + q + 1, :] = row[:, 128 * q : 128 * (q + 1)]


def inverse(x):
    return pl.reciprocal(x, approx=True)


def kernel(
    sizes,
    slip_hbm,
    log_state_hbm,
    friction_a_hbm,
    friction_b_hbm,
    stress_hbm,
    leak_hbm,
    corner_hbm,
    fraction_hbm,
    row_basis_hbm,
    col_basis_hbm,
    far_row_hbm,
    far_col_hbm,
    far_rank_hbm,
    table_hbm,
    near_hbm,
    coupling_hbm,
    p_hbm,
    region_hbm,
    rate_hbm,
    accel_out,
    state_out,
    slip,
    log_state,
    friction_a,
    friction_b,
    stress,
    leak,
    corner,
    fraction,
    row_basis,
    col_basis,
    far_row,
    far_col,
    far_rank,
    table,
    pv,
    rv,
    region,
    acc,
    source,
    snd,
    rcv,
    fsnd,
    frcv,
    p_edge,
    r_edge,
    wz,
    wyx,
    p_low,
    near,
    coupling,
    pick,
    gather_x,
    gather,
    slip_edge,
    window,
    flow_row,
    fp_row,
    fp_own,
    fp_other,
    near_own,
    near_other,
    tot_own,
    tot_other,
    block,
    far16,
    load_sem,
    x_send,
    x_recv,
    z_send,
    z_recv,
    y_send,
    y_recv,
    pr_send,
    pr_recv,
    fl_send,
    fl_recv,
    one_send,
    one_recv,
    out_sem,
):
    ny, nz, nx = sizes
    slabs = ny * nz * nx
    planes, width_y, width_z = region.shape
    half = width_y // 2
    rows = half // PARTS
    rank = col_basis.shape[0]
    cells = corner.shape[1]
    yi, zi, xi = (lax.axis_index(name) for name in SLAB)
    bi = lax.axis_index("blk")
    slab = (yi * nz + zi) * nx + xi

    def chip_of(index):
        return (
            lax.div(index, nz * nx),
            lax.rem(lax.div(index, nx), nz),
            lax.rem(index, nx),
            bi,
        )

    above = chip_of(lax.rem(slab + 1, slabs))
    below = chip_of(lax.rem(slab + slabs - 1, slabs))
    other = (yi, zi, xi, 1 - bi)
    x_peers = [(yi, zi, lax.rem(xi + d, nx), bi) for d in range(1, nx)]
    z_peers = [(yi, lax.rem(zi + d, nz), xi, bi) for d in range(1, nz)]
    y_peers = [(lax.rem(yi + d, ny), zi, xi, bi) for d in range(1, ny)]

    barrier = pltpu.get_barrier_semaphore()
    peers = [above, below, other] + x_peers + z_peers + y_peers
    for peer in peers:
        pl.semaphore_signal(barrier, inc=1, device_id=peer, device_id_type=MESH)

    def remote(src, dst, send, recv, device):
        return pltpu.make_async_remote_copy(
            src_ref=src,
            dst_ref=dst,
            send_sem=send,
            recv_sem=recv,
            device_id=device,
            device_id_type=MESH,
        )

    def quarter(plane, part, sem):
        at = pl.ds(part * half, half)
        to = pl.ds(HALO + part * half, half)
        return (
            pltpu.make_async_copy(
                region_hbm.at[plane, at], region.at[plane, at], load_sem.at[sem]
            ),
            pltpu.make_async_copy(p_hbm.at[plane, at], pv.at[plane, to], load_sem.at[sem + 1]),
        )

    first_up, first_down = quarter(1, 0, 0), quarter(0, 1, 2)
    later = quarter(0, 0, 4) + quarter(1, 1, 6)
    small = [
        pltpu.make_async_copy(src, dst, load_sem.at[10 + i])
        for i, (src, dst) in enumerate(
            (
                (slip_hbm, slip),
                (col_basis_hbm, col_basis),
                (table_hbm, table),
                (leak_hbm, leak),
                (corner_hbm, corner),
                (fraction_hbm, fraction),
                (far_col_hbm, far_col),
                (far_rank_hbm, far_rank),
                (far_row_hbm, far_row),
                (row_basis_hbm, row_basis),
                (stress_hbm, stress),
                (log_state_hbm, log_state),
                (friction_a_hbm, friction_a),
                (friction_b_hbm, friction_b),
            )
        )
    ]
    load_near = pltpu.make_async_copy(near_hbm, near, load_sem.at[8])
    load_coupling = pltpu.make_async_copy(coupling_hbm, coupling, load_sem.at[9])
    ahead = small[:4]
    behind = small[4:6]
    last = small[6:]
    for copy in ahead[:3] + list(first_up + first_down) + ahead[3:] + behind + list(later):
        copy.start()
    for copy in [load_near, load_coupling] + last:
        copy.start()
    for copy in ahead:
        copy.wait()

    for c in range(4):
        window[1 + c : 2 + c, :] = lanes_row(slip, 4 * c, 4)
    slip_row = jnp.concatenate([window[1 + c : 2 + c, :] for c in range(4)], axis=1)
    spread = jnp.broadcast_to(slip_row, (8, cells))
    lane = lax.broadcasted_iota(jnp.int32, (8, cells), 1)
    sub = lax.broadcasted_iota(jnp.int32, (8, cells), 0)
    spread = jnp.where(
        (lane >= sub * 512) & (lane < sub * 512 + 512), spread, jnp.float32(0.0)
    ).astype(jnp.bfloat16)
    moments = lax.dot_general(
        spread, col_basis[...], (((1,), (1,)), ((), ())), preferred_element_type=jnp.float32
    )
    gather_x[xi] = jnp.zeros((8, 128), jnp.float32)
    gather_x[xi, :, 0:rank] = moments
    for c in range(16):
        flow_row[:, 128 * c : 128 * (c + 1)] = leak[c : c + 1, :] * slip[c : c + 1, :]

    pl.semaphore_wait(barrier, len(peers))

    x_copies = [
        remote(gather_x.at[xi], gather_x.at[xi], x_send.at[d], x_recv.at[d], peer)
        for d, peer in enumerate(x_peers)
    ]
    for copy in x_copies:
        copy.start()
    slip_up = remote(slip.at[8:16], slip_edge.at[0], one_send.at[0], one_recv.at[0], above)
    slip_down = remote(slip.at[0:8], slip_edge.at[1], one_send.at[1], one_recv.at[1], below)
    slip_up.start()
    slip_down.start()

    halves = jnp.concatenate([0.5 / table[...], jnp.zeros((1, 128 - table.shape[1]), jnp.float32)], axis=1)

    def look_up(plane, start, count):
        chosen = region[plane, pl.ds(start, count), :]
        entries = jnp.broadcast_to(halves, (count, 128))
        r = jnp.concatenate(
            [
                jnp.take_along_axis(
                    entries,
                    chosen[:, 128 * j : 128 * (j + 1)],
                    axis=1,
                    mode="promise_in_bounds",
                )
                for j in range(width_z // 128)
            ],
            axis=1,
        )
        p = pv[plane, pl.ds(HALO + start, count), :].astype(jnp.bfloat16)
        rv[plane, pl.ds(HALO + start, count), :] = r
        p_low[pl.ds(plane * width_y + start, count), :] = p
        return p, r.astype(jnp.bfloat16)

    pr_copies = []
    for part in range(PARTS):
        for way, plane, offset, device, loads in (
            (0, 1, 0, above, first_up),
            (1, 0, half, below, first_down),
        ):
            if part == 0:
                for copy in loads:
                    copy.wait()
            p, r = look_up(plane, offset + part * rows, rows)
            snd[way, part, 0] = p
            snd[way, part, 1] = r
            copy = remote(
                snd.at[way, part],
                rcv.at[way, part],
                pr_send.at[way, part],
                pr_recv.at[way, part],
                device,
            )
            copy.start()
            pr_copies.append(copy)

    for copy in later + tuple(behind):
        copy.wait()

    def rest(step, carry):
        start = pl.multiple_of(step * rows, rows)
        look_up(0, start, rows)
        look_up(1, start + half, rows)
        return carry

    lax.fori_loop(0, PARTS, rest, 0)

    edge = pl.multiple_of(HALO + (1 - bi) * (width_y - 8), 8)
    p_copy = remote(
        pv.at[:, pl.ds(edge, 8), :], p_edge, one_send.at[2], one_recv.at[2], other
    )
    r_copy = remote(
        rv.at[:, pl.ds(edge, 8), :], r_edge, one_send.at[3], one_recv.at[3], other
    )
    p_copy.start()
    r_copy.start()

    y_start = bi * width_y

    def sample(step, carry):
        at = pl.ds(pl.multiple_of(step * F_TILE, F_TILE), F_TILE)
        z = corner[2:3, at]
        fz = fraction[2:3, at]
        iota = lax.broadcasted_iota(jnp.int16, (width_z, F_TILE), 0)
        z = jnp.broadcast_to(z, (16, F_TILE)).astype(jnp.int16)[0:1]
        weight = jnp.where(
            iota == z,
            (1.0 - fz).astype(jnp.bfloat16),
            jnp.where(iota == z + 1, fz.astype(jnp.bfloat16), jnp.bfloat16(0.0)),
        )
        wz[:, at] = weight
        along_z = jnp.dot(p_low[...], weight, preferred_element_type=jnp.float32)
        y = corner[1:2, at] - y_start
        fy = fraction[1:2, at]
        fx = fraction[0:1, at]
        flow = flow_row[:, at]
        iota = lax.broadcasted_iota(jnp.int32, (width_y, F_TILE), 0)
        weight_y = jnp.where(iota == y, 1.0 - fy, jnp.where(iota == y + 1, fy, jnp.float32(0.0)))
        low = jnp.sum(along_z[:width_y] * weight_y, axis=0, keepdims=True)
        high = jnp.sum(along_z[width_y:] * weight_y, axis=0, keepdims=True)
        fp_row[:, at] = (1.0 - fx) * low + fx * high
        wyx[0:width_y, at] = (weight_y * ((1.0 - fx) * flow)).astype(jnp.bfloat16)
        wyx[width_y:, at] = (weight_y * (fx * flow)).astype(jnp.bfloat16)
        return carry

    steps = cells // F_TILE
    lax.fori_loop(0, 1, sample, 0)

    for copy in x_copies:
        copy.wait_recv()
    mine = jnp.concatenate([gather_x[i, 0:4, :] for i in range(nx)], axis=0)
    gather[yi, zi] = mine.astype(jnp.bfloat16)
    z_copies = [
        remote(gather.at[yi, zi], gather.at[yi, zi], z_send.at[d], z_recv.at[d], peer)
        for d, peer in enumerate(z_peers)
    ]
    for copy in z_copies:
        copy.start()

    has_below = jnp.where(slab > 0, 1.0, 0.0).astype(jnp.float32)
    has_above = jnp.where(slab < slabs - 1, 1.0, 0.0).astype(jnp.float32)
    fl_copies = {}

    def faces(part):
        for way, plane, offset, device, present in (
            (0, 0, 0, below, has_below),
            (1, 1, half, above, has_above),
        ):
            pr_copies[2 * part + way].wait_recv()
            at = pl.ds(HALO + offset + part * rows, rows)
            p_in = rcv[way, part, 0].astype(jnp.float32)
            r_in = rcv[way, part, 1].astype(jnp.float32)
            drop = pv[plane, at, :] - p_in
            flux = drop * (inverse(rv[plane, at, :] + r_in) * -present)
            fsnd[way, part] = flux.astype(jnp.bfloat16)
            copy = remote(
                fsnd.at[way, part],
                frcv.at[way, part],
                fl_send.at[way, part],
                fl_recv.at[way, part],
                device,
            )
            copy.start()
            fl_copies[way, part] = copy

    lax.fori_loop(1, 3, sample, 0)
    faces(0)
    lax.fori_loop(3, steps, sample, 0)
    for c in range(16):
        fp_own[c : c + 1, :] = fp_row[:, 128 * c : 128 * (c + 1)]
    fp_copy = remote(fp_own, fp_other, one_send.at[4], one_recv.at[4], other)
    fp_copy.start()

    for copy in z_copies:
        copy.wait_recv()
    y_copies = [
        remote(gather.at[yi], gather.at[yi], y_send.at[d], y_recv.at[d], peer)
        for d, peer in enumerate(y_peers)
    ]
    for copy in y_copies:
        copy.start()

    slip_up.wait_recv()
    slip_down.wait_recv()
    window[0:1, :] = has_below * jnp.concatenate(
        [slip_edge[0, 4 + q : 5 + q, :] for q in range(4)], axis=1
    )
    window[5:6, :] = has_above * jnp.concatenate(
        [slip_edge[1, q : 1 + q, :] for q in range(4)], axis=1
    )
    load_near.wait()
    for i in range(2):
        total = jnp.zeros((8, 512), jnp.float32)
        for j in range(3):
            row = window[pl.ds(2 * bi + i + j, 1), :]
            row = jnp.broadcast_to(row, (8, 512)).astype(jnp.bfloat16)
            total = total + lax.dot_general(
                row, near[i, j], (((1,), (1,)), ((), ())), preferred_element_type=jnp.float32
            )
        store_rows(near_own, 4 * i, total[0:1, :])
    near_copy = remote(near_own, near_other, one_send.at[5], one_recv.at[5], other)
    near_copy.start()
    faces(1)

    p_copy.wait_recv()
    r_copy.wait_recv()
    inner = (1 - bi).astype(jnp.float32)
    for plane in range(planes):
        p_lower, r_lower = p_edge[plane, 7:8, :], r_edge[plane, 7:8, :]
        p_upper, r_upper = p_edge[plane, 0:1, :], r_edge[plane, 0:1, :]
        pv[plane, 7:8, :] = p_lower
        rv[plane, 7:8, :] = r_lower + inner * FAR
        pv[plane, HALO + width_y : HALO + width_y + 1, :] = p_upper
        rv[plane, HALO + width_y : HALO + width_y + 1, :] = r_upper + (1.0 - inner) * FAR

    def stencil(y):
        p = [pv[plane, pl.ds(HALO + y, 8), :] for plane in range(planes)]
        r = [rv[plane, pl.ds(HALO + y, 8), :] for plane in range(planes)]
        last = lax.broadcasted_iota(jnp.int32, (8, width_z), 1) == width_z - 1
        between = (p[1] - p[0]) * inverse(r[0] + r[1])
        for plane in range(planes):
            pc, rc = p[plane], r[plane]
            total = between if plane == 0 else -between
            for shift in (1, -1):
                pn = pv.at[plane, pl.ds(y, 24), :][HALO + shift : HALO + shift + 8, :]
                rn = rv.at[plane, pl.ds(y, 24), :][HALO + shift : HALO + shift + 8, :]
                total = total + (pn - pc) * inverse(rn + rc)
            pn = pltpu.roll(pc, width_z - 1, 1)
            rn = pltpu.roll(rc, width_z - 1, 1)
            flux = jnp.where(last, jnp.float32(0.0), (pn - pc) * inverse(rn + rc))
            total = total + flux - pltpu.roll(flux, 1, 1)
            acc[plane, pl.ds(y, 8), :] = total

    def spread_source(step, carry):
        at = pl.ds(pl.multiple_of(step * Z_TILE, Z_TILE), Z_TILE)
        result = lax.dot_general(
            wyx[...], wz[at, :], (((1,), (1,)), ((), ())), preferred_element_type=jnp.float32
        )
        source[0, :, at] = result[:width_y]
        source[1, :, at] = result[width_y:]
        count = width_y // 8 // (width_z // Z_TILE)
        for k in range(count):
            stencil(pl.multiple_of((step * count + k) * 8, 8))
        return carry

    spreads = width_z // Z_TILE
    lax.fori_loop(0, spreads // 2, spread_source, 0)
    faces(2)
    faces(3)

    for copy in last:
        copy.wait()
    column = lanes_row(far_col, 0, 8)
    pick[...] = jnp.where(
        lax.broadcasted_iota(jnp.int32, pick.shape, 0) == column, 1.0, 0.0
    ).astype(jnp.bfloat16)
    for copy in y_copies:
        copy.wait_recv()
    moments = gather[...].reshape(512, 128)[:, 0:rank]
    picked = lax.dot_general(
        moments, pick[...], (((0,), (0,)), ((), ())), preferred_element_type=jnp.float32
    )
    ranks = lanes_row(far_rank, 0, 8)
    masked = jnp.where(
        lax.broadcasted_iota(jnp.int32, picked.shape, 0) < ranks, picked, jnp.float32(0.0)
    )
    load_coupling.wait()
    for a in range(rank):
        block[a : a + 1, :] = jnp.sum(
            coupling[a].astype(jnp.float32) * masked, axis=0, keepdims=True
        )
    target = lanes_row(far_row, 0, 8)
    lane = lax.broadcasted_iota(jnp.int32, (rank, 128), 1)
    totals = jnp.zeros((rank, 128), jnp.float32)
    for c in range(4):
        share = jnp.sum(
            jnp.where(target == c, block[...], jnp.float32(0.0)), axis=1, keepdims=True
        )
        totals = totals + jnp.where(lane == c, share, jnp.float32(0.0))
    tot_own[...] = totals
    tot_copy = remote(tot_own, tot_other, one_send.at[6], one_recv.at[6], other)
    tot_copy.start()

    lax.fori_loop(spreads // 2, spreads, spread_source, 0)

    tot_copy.wait_recv()
    near_copy.wait_recv()
    fp_copy.wait_recv()
    totals = tot_own[...] + tot_other[...]
    for c in range(4):
        basis = row_basis[:, 512 * c : 512 * (c + 1)].astype(jnp.float32)
        store_rows(
            far16, 4 * c, jnp.sum(basis * totals[:, c : c + 1], axis=0, keepdims=True)
        )
    own, others = near_own[...], near_other[...]
    first = bi == 0
    near16 = jnp.concatenate(
        [jnp.where(first, own, others), jnp.where(first, others, own)], axis=0
    )
    traction = near16 + far16[...]
    effective = stress[...] - (fp_own[...] + fp_other[...])
    rate = slip[...]
    state_rate = jnp.exp(-log_state[...]) - rate
    accel_out[...] = (traction - effective * friction_b[...] * state_rate) / (
        effective * friction_a[...] / rate + 0.5
    )
    state_out[...] = state_rate

    stores = []
    for part in range(PARTS):
        low = pl.ds(part * rows, rows)
        high = pl.ds(half + part * rows, rows)
        for which, plane, at, flux in (
            (0, 0, low, fsnd.at[0, part]),
            (1, 1, high, fsnd.at[1, part]),
        ):
            value = flux[...].astype(jnp.float32)
            acc[plane, at, :] = acc[plane, at, :] + source[plane, at, :] + value
            copy = pltpu.make_async_copy(
                acc.at[plane, at], rate_hbm.at[plane, at], out_sem.at[which, part]
            )
            copy.start()
            stores.append(copy)
    for part in range(PARTS):
        low = pl.ds(part * rows, rows)
        high = pl.ds(half + part * rows, rows)
        for which, plane, at, way in ((2, 1, low, 0), (3, 0, high, 1)):
            fl_copies[way, part].wait_recv()
            value = frcv[way, part].astype(jnp.float32)
            acc[plane, at, :] = acc[plane, at, :] + source[plane, at, :] - value
            copy = pltpu.make_async_copy(
                acc.at[plane, at], rate_hbm.at[plane, at], out_sem.at[which, part]
            )
            copy.start()
            stores.append(copy)
    for copy in stores:
        copy.wait()
    sent = x_copies + z_copies + y_copies + pr_copies + list(fl_copies.values())
    for copy in sent + [slip_up, slip_down, p_copy, r_copy, fp_copy, near_copy, tot_copy]:
        copy.wait_send()


def hand_over(rate_in, accel_in, state_in, rate, accel, state, held, held_two, sem):
    planes, width_y, _ = rate.shape
    part = width_y // 4
    ways = [(accel_in, held_two.at[0], accel), (state_in, held_two.at[1], state)]
    for plane in range(planes):
        for k in range(4):
            at = (plane, pl.ds(part * k, part))
            ways.append((rate_in.at[at], held.at[at], rate.at[at]))
    loads = [
        pltpu.make_async_copy(src, mid, sem.at[0, i]) for i, (src, mid, _) in enumerate(ways)
    ]
    stores = [
        pltpu.make_async_copy(mid, dst, sem.at[1, i]) for i, (_, mid, dst) in enumerate(ways)
    ]
    for load in loads:
        load.start()
    for load, store in zip(loads, stores):
        load.wait()
        store.start()
    for store in stores:
        store.wait()


def shards(
    slip_rate,
    log_state,
    friction_a,
    friction_b,
    normal_stress,
    leak_rate,
    corner,
    fraction,
    near_blocks,
    row_basis,
    col_basis,
    far_row,
    far_col,
    far_rank,
    far_coupling,
    pressure,
    region,
    perm_table,
):
    sizes = tuple(lax.axis_size(name) for name in SLAB)
    ny, nz, nx = sizes
    planes, width_y, width_z = pressure.shape
    cells = slip_rate.shape[0]
    clusters = cells // 512
    slots = far_row.shape[0]
    rank = col_basis.shape[0]
    rows = width_y // 2 // PARTS
    f32, bf16 = jnp.float32, jnp.bfloat16
    vmem = pl.BlockSpec(memory_space=pltpu.VMEM)
    hbm = pl.BlockSpec(memory_space=pl.ANY)
    dma = pltpu.SemaphoreType.DMA

    def cut(x):
        return x.reshape(-1, 128)

    shapes = (
        jax.ShapeDtypeStruct(pressure.shape, f32),
        jax.ShapeDtypeStruct((cells // 128, 128), f32),
        jax.ShapeDtypeStruct((cells // 128, 128), f32),
    )
    results = pl.pallas_call(
        functools.partial(kernel, sizes),
        out_shape=shapes,
        in_specs=[hbm] * 18,
        out_specs=(hbm, vmem, vmem),
        scratch_shapes=[
            *[pltpu.VMEM((cells // 128, 128), f32)] * 6,
            pltpu.VMEM(corner.shape, jnp.int32),
            pltpu.VMEM(fraction.shape, f32),
            pltpu.VMEM(row_basis.shape, bf16),
            pltpu.VMEM(col_basis.shape, bf16),
            *[pltpu.VMEM((slots // 128, 128), jnp.int32)] * 3,
            pltpu.VMEM((1, perm_table.shape[0]), f32),
            pltpu.VMEM((planes, width_y + 2 * HALO, width_z), f32),
            pltpu.VMEM((planes, width_y + 2 * HALO, width_z), f32),
            pltpu.VMEM((planes, width_y, width_z), jnp.int32),
            pltpu.VMEM((planes, width_y, width_z), f32),
            pltpu.VMEM((planes, width_y, width_z), f32),
            pltpu.VMEM((2, PARTS, 2, rows, width_z), bf16),
            pltpu.VMEM((2, PARTS, 2, rows, width_z), bf16),
            pltpu.VMEM((2, PARTS, rows, width_z), bf16),
            pltpu.VMEM((2, PARTS, rows, width_z), bf16),
            pltpu.VMEM((planes, 8, width_z), f32),
            pltpu.VMEM((planes, 8, width_z), f32),
            pltpu.VMEM((width_z, cells), bf16),
            pltpu.VMEM((planes * width_y, cells), bf16),
            pltpu.VMEM((planes * width_y, width_z), bf16),
            pltpu.VMEM(near_blocks.shape, bf16),
            pltpu.VMEM(far_coupling.shape, bf16),
            pltpu.VMEM((ny * nz * nx * clusters, slots), bf16),
            pltpu.VMEM((nx, 8, 128), f32),
            pltpu.VMEM((ny, nz, nx * clusters, 128), bf16),
            pltpu.VMEM((2, 8, 128), f32),
            pltpu.VMEM((8, 512), f32),
            pltpu.VMEM((1, cells), f32),
            pltpu.VMEM((1, cells), f32),
            pltpu.VMEM((cells // 128, 128), f32),
            pltpu.VMEM((cells // 128, 128), f32),
            pltpu.VMEM((8, 128), f32),
            pltpu.VMEM((8, 128), f32),
            pltpu.VMEM((rank, 128), f32),
            pltpu.VMEM((rank, 128), f32),
            pltpu.VMEM((rank, slots), f32),
            pltpu.VMEM((cells // 128, 128), f32),
            dma((24,)),
            dma((nx - 1,)),
            dma((nx - 1,)),
            dma((nz - 1,)),
            dma((nz - 1,)),
            dma((ny - 1,)),
            dma((ny - 1,)),
            dma((2, PARTS)),
            dma((2, PARTS)),
            dma((2, PARTS)),
            dma((2, PARTS)),
            dma((7,)),
            dma((7,)),
            dma((4, PARTS)),
        ],
        compiler_params=pltpu.CompilerParams(
            collective_id=0, has_side_effects=True, vmem_limit_bytes=60 * 1024 * 1024
        ),
        name="fault_step",
    )(
        cut(slip_rate),
        cut(log_state),
        cut(friction_a),
        cut(friction_b),
        cut(normal_stress),
        cut(leak_rate),
        corner,
        fraction,
        row_basis,
        col_basis,
        cut(far_row),
        cut(far_col),
        cut(far_rank),
        perm_table.reshape(1, -1),
        near_blocks,
        far_coupling,
        pressure,
        region,
    )
    rate, accel, state = pl.pallas_call(
        hand_over,
        out_shape=shapes,
        in_specs=[hbm] * 3,
        out_specs=(hbm,) * 3,
        scratch_shapes=[
            pltpu.VMEM(pressure.shape, f32),
            pltpu.VMEM((2, cells // 128, 128), f32),
            dma((2, 10)),
        ],
        compiler_params=pltpu.CompilerParams(vmem_limit_bytes=60 * 1024 * 1024),
        name="hand_over",
    )(*results)
    return accel.reshape(cells), state.reshape(cells), rate


def solution(mesh):
    torus = Mesh(
        mesh.devices.reshape(4, 8, 4, mesh.shape["blk"]), ("slab_0", "slab_1", "slab_2", "blk")
    )
    placed = (
        P(SLAB),
        P(SLAB),
        P(SLAB),
        P(SLAB),
        P(SLAB),
        P(SLAB),
        P(None, SLAB),
        P(None, SLAB),
        P(SLAB_BLK, None, None, None),
        P(None, SLAB),
        P(None, SLAB),
        P(SLAB_BLK),
        P(SLAB_BLK),
        P(SLAB_BLK),
        P(None, None, SLAB_BLK),
        P(SLAB, "blk", None),
        P(SLAB, "blk", None),
        P(),
    )
    return jax.shard_map(
        shards,
        mesh=torus,
        in_specs=placed,
        out_specs=(P(SLAB), P(SLAB), P(SLAB, "blk", None)),
        check_vma=False,
    )
```

```python
import functools

import jax
import jax.numpy as jnp
from jax import lax
from jax.experimental import pallas as pl
from jax.experimental.pallas import tpu as pltpu
from jax.sharding import Mesh
from jax.sharding import PartitionSpec as P

SLAB = ("slab_0", "slab_1", "slab_2")
SLAB_BLK = ("slab_0", "slab_1", "slab_2", "blk")
MESH = pl.DeviceIdType.MESH

PARTS = 4
F_TILE = 512
Z_TILE = 256
HALO = 8
FAR = 1e30


def lanes_row(ref, first, count):
    return jnp.concatenate([ref[first + q : first + q + 1, :] for q in range(count)], axis=1)


def store_rows(ref, first, row):
    for q in range(row.shape[1] // 128):
        ref[first + q : first + q + 1, :] = row[:, 128 * q : 128 * (q + 1)]


def inverse(x):
    return pl.reciprocal(x, approx=True)


def kernel(
    sizes,
    slip_hbm,
    log_state_hbm,
    friction_a_hbm,
    friction_b_hbm,
    stress_hbm,
    leak_hbm,
    corner_hbm,
    fraction_hbm,
    row_basis_hbm,
    col_basis_hbm,
    far_row_hbm,
    far_col_hbm,
    far_rank_hbm,
    table_hbm,
    near_hbm,
    coupling_hbm,
    p_hbm,
    region_hbm,
    rate_hbm,
    accel_out,
    state_out,
    slip,
    log_state,
    friction_a,
    friction_b,
    stress,
    leak,
    corner,
    fraction,
    row_basis,
    col_basis,
    far_row,
    far_col,
    far_rank,
    table,
    pv,
    rv,
    region,
    acc,
    source,
    snd,
    rcv,
    fsnd,
    frcv,
    p_edge,
    r_edge,
    wz,
    wyx,
    p_low,
    near,
    coupling,
    pick,
    gather_xy,
    gather,
    slip_edge,
    window,
    flow_row,
    fp_row,
    fp_own,
    fp_other,
    near_own,
    near_other,
    tot_own,
    tot_other,
    block,
    far16,
    load_sem,
    xy_send,
    xy_recv,
    z_send,
    z_recv,
    pr_send,
    pr_recv,
    fl_send,
    fl_recv,
    one_send,
    one_recv,
    out_sem,
):
    ny, nz, nx = sizes
    slabs = ny * nz * nx
    planes, width_y, width_z = region.shape
    half = width_y // 2
    rows = half // PARTS
    rank = col_basis.shape[0]
    cells = corner.shape[1]
    yi, zi, xi = (lax.axis_index(name) for name in SLAB)
    bi = lax.axis_index("blk")
    slab = (yi * nz + zi) * nx + xi

    def chip_of(index):
        return (
            lax.div(index, nz * nx),
            lax.rem(lax.div(index, nx), nz),
            lax.rem(index, nx),
            bi,
        )

    above = chip_of(lax.rem(slab + 1, slabs))
    below = chip_of(lax.rem(slab + slabs - 1, slabs))
    other = (yi, zi, xi, 1 - bi)
    xy_peers = [
        (lax.rem(yi + dy, ny), zi, lax.rem(xi + dx, nx), bi)
        for dy in range(ny)
        for dx in range(nx)
        if dy or dx
    ]
    z_peers = [(yi, lax.rem(zi + d, nz), xi, bi) for d in range(1, nz)]
    has_below, has_above = slab > 0, slab < slabs - 1

    barrier = pltpu.get_barrier_semaphore()
    peers = [above, below, other] + xy_peers + z_peers
    for peer in peers:
        pl.semaphore_signal(barrier, inc=1, device_id=peer, device_id_type=MESH)

    def remote(src, dst, send, recv, device):
        return pltpu.make_async_remote_copy(
            src_ref=src,
            dst_ref=dst,
            send_sem=send,
            recv_sem=recv,
            device_id=device,
            device_id_type=MESH,
        )

    def quarter(plane, part, sem):
        at = pl.ds(part * half, half)
        to = pl.ds(HALO + part * half, half)
        return (
            pltpu.make_async_copy(
                region_hbm.at[plane, at], region.at[plane, at], load_sem.at[sem]
            ),
            pltpu.make_async_copy(p_hbm.at[plane, at], pv.at[plane, to], load_sem.at[sem + 1]),
        )

    first_up, first_down = quarter(1, 0, 0), quarter(0, 1, 2)
    later = quarter(0, 0, 4) + quarter(1, 1, 6)
    small = [
        pltpu.make_async_copy(src, dst, load_sem.at[10 + i])
        for i, (src, dst) in enumerate(
            (
                (slip_hbm, slip),
                (col_basis_hbm, col_basis),
                (table_hbm, table),
                (leak_hbm, leak),
                (corner_hbm, corner),
                (fraction_hbm, fraction),
                (far_col_hbm, far_col),
                (far_rank_hbm, far_rank),
                (far_row_hbm, far_row),
                (row_basis_hbm, row_basis),
                (stress_hbm, stress),
                (log_state_hbm, log_state),
                (friction_a_hbm, friction_a),
                (friction_b_hbm, friction_b),
            )
        )
    ]
    load_near = pltpu.make_async_copy(near_hbm, near, load_sem.at[8])
    load_coupling = pltpu.make_async_copy(coupling_hbm, coupling, load_sem.at[9])
    ahead = small[:4]
    behind = small[4:6]
    last = small[6:]
    for copy in ahead[:3] + list(first_up + first_down) + ahead[3:] + behind + list(later):
        copy.start()
    for copy in [load_near, load_coupling] + last:
        copy.start()
    for copy in ahead:
        copy.wait()

    for c in range(4):
        window[1 + c : 2 + c, :] = lanes_row(slip, 4 * c, 4)
    slip_row = jnp.concatenate([window[1 + c : 2 + c, :] for c in range(4)], axis=1)
    spread = jnp.broadcast_to(slip_row, (8, cells))
    lane = lax.broadcasted_iota(jnp.int32, (8, cells), 1)
    sub = lax.broadcasted_iota(jnp.int32, (8, cells), 0)
    spread = jnp.where(
        (lane >= sub * 512) & (lane < sub * 512 + 512), spread, jnp.float32(0.0)
    ).astype(jnp.bfloat16)
    moments = lax.dot_general(
        spread, col_basis[...], (((1,), (1,)), ((), ())), preferred_element_type=jnp.float32
    )
    gather_xy[yi, xi] = jnp.zeros((8, 128), jnp.float32)
    gather_xy[yi, xi, :, 0:rank] = moments
    for c in range(16):
        flow_row[:, 128 * c : 128 * (c + 1)] = leak[c : c + 1, :] * slip[c : c + 1, :]

    pl.semaphore_wait(barrier, len(peers))

    xy_copies = [
        remote(gather_xy.at[yi, xi], gather_xy.at[yi, xi], xy_send.at[d], xy_recv.at[d], peer)
        for d, peer in enumerate(xy_peers)
    ]
    for copy in xy_copies:
        copy.start()
    slip_up = remote(slip.at[8:16], slip_edge.at[0], one_send.at[0], one_recv.at[0], above)
    slip_down = remote(slip.at[0:8], slip_edge.at[1], one_send.at[1], one_recv.at[1], below)
    slip_up.start()
    slip_down.start()

    halves = jnp.concatenate([0.5 / table[...], jnp.zeros((1, 128 - table.shape[1]), jnp.float32)], axis=1)

    def look_up(plane, start, count):
        chosen = region[plane, pl.ds(start, count), :]
        entries = jnp.broadcast_to(halves, (count, 128))
        r = jnp.concatenate(
            [
                jnp.take_along_axis(
                    entries,
                    chosen[:, 128 * j : 128 * (j + 1)],
                    axis=1,
                    mode="promise_in_bounds",
                )
                for j in range(width_z // 128)
            ],
            axis=1,
        )
        p = pv[plane, pl.ds(HALO + start, count), :].astype(jnp.bfloat16)
        rv[plane, pl.ds(HALO + start, count), :] = r
        p_low[pl.ds(plane * width_y + start, count), :] = p
        return p, r.astype(jnp.bfloat16)

    pr_copies = []
    for part in range(PARTS):
        for way, plane, offset, device, loads, present in (
            (0, 1, 0, above, first_up, has_above),
            (1, 0, half, below, first_down, has_below),
        ):
            if part == 0:
                for copy in loads:
                    copy.wait()
            p, r = look_up(plane, offset + part * rows, rows)
            snd[way, part, 0] = p
            snd[way, part, 1] = r
            copy = remote(
                snd.at[way, part],
                rcv.at[way, part],
                pr_send.at[way, part],
                pr_recv.at[way, part],
                device,
            )
            pl.when(present)(copy.start)
            pr_copies.append(copy)

    for copy in later + tuple(behind):
        copy.wait()

    def rest(step, carry):
        start = pl.multiple_of(step * rows, rows)
        look_up(0, start, rows)
        look_up(1, start + half, rows)
        return carry

    lax.fori_loop(0, PARTS, rest, 0)

    edge = pl.multiple_of(HALO + (1 - bi) * (width_y - 8), 8)
    p_copy = remote(
        pv.at[:, pl.ds(edge, 8), :], p_edge, one_send.at[2], one_recv.at[2], other
    )
    r_copy = remote(
        rv.at[:, pl.ds(edge, 8), :], r_edge, one_send.at[3], one_recv.at[3], other
    )
    p_copy.start()
    r_copy.start()

    y_start = bi * width_y

    def sample(step, carry):
        at = pl.ds(pl.multiple_of(step * F_TILE, F_TILE), F_TILE)
        z = corner[2:3, at]
        fz = fraction[2:3, at]
        iota = lax.broadcasted_iota(jnp.int16, (width_z, F_TILE), 0)
        z = jnp.broadcast_to(z, (16, F_TILE)).astype(jnp.int16)[0:1]
        weight = jnp.where(
            iota == z,
            (1.0 - fz).astype(jnp.bfloat16),
            jnp.where(iota == z + 1, fz.astype(jnp.bfloat16), jnp.bfloat16(0.0)),
        )
        wz[:, at] = weight
        along_z = jnp.dot(p_low[...], weight, preferred_element_type=jnp.float32)
        y = corner[1:2, at] - y_start
        fy = fraction[1:2, at]
        fx = fraction[0:1, at]
        flow = flow_row[:, at]
        iota = lax.broadcasted_iota(jnp.int32, (width_y, F_TILE), 0)
        weight_y = jnp.where(iota == y, 1.0 - fy, jnp.where(iota == y + 1, fy, jnp.float32(0.0)))
        low = jnp.sum(along_z[:width_y] * weight_y, axis=0, keepdims=True)
        high = jnp.sum(along_z[width_y:] * weight_y, axis=0, keepdims=True)
        fp_row[:, at] = (1.0 - fx) * low + fx * high
        wyx[0:width_y, at] = (weight_y * ((1.0 - fx) * flow)).astype(jnp.bfloat16)
        wyx[width_y:, at] = (weight_y * (fx * flow)).astype(jnp.bfloat16)
        return carry

    steps = cells // F_TILE
    lax.fori_loop(0, 1, sample, 0)

    for copy in xy_copies:
        copy.wait_recv()
    mine = jnp.concatenate(
        [gather_xy[j, i, 0:4, :] for j in range(ny) for i in range(nx)], axis=0
    )
    gather[zi] = mine.astype(jnp.bfloat16)
    z_copies = [
        remote(gather.at[zi], gather.at[zi], z_send.at[d], z_recv.at[d], peer)
        for d, peer in enumerate(z_peers)
    ]
    for copy in z_copies:
        copy.start()

    fl_copies = {}

    def faces(part):
        for way, plane, offset, device, present in (
            (0, 0, 0, below, has_below),
            (1, 1, half, above, has_above),
        ):
            copy = remote(
                fsnd.at[way, part],
                frcv.at[way, part],
                fl_send.at[way, part],
                fl_recv.at[way, part],
                device,
            )
            fl_copies[way, part] = copy

            @pl.when(present)
            def _(way=way, plane=plane, offset=offset, copy=copy):
                pr_copies[2 * part + way].wait_recv()
                at = pl.ds(HALO + offset + part * rows, rows)
                p_in = rcv[way, part, 0].astype(jnp.float32)
                r_in = rcv[way, part, 1].astype(jnp.float32)
                drop = p_in - pv[plane, at, :]
                flux = drop * inverse(rv[plane, at, :] + r_in)
                fsnd[way, part] = flux.astype(jnp.bfloat16)
                copy.start()

            @pl.when(jnp.logical_not(present))
            def _(way=way):
                fsnd[way, part] = jnp.zeros((rows, width_z), jnp.bfloat16)
                frcv[1 - way, part] = jnp.zeros((rows, width_z), jnp.bfloat16)

    lax.fori_loop(1, 3, sample, 0)
    faces(0)
    lax.fori_loop(3, steps, sample, 0)
    for c in range(16):
        fp_own[c : c + 1, :] = fp_row[:, 128 * c : 128 * (c + 1)]
    fp_copy = remote(fp_own, fp_other, one_send.at[4], one_recv.at[4], other)
    fp_copy.start()

    slip_up.wait_recv()
    slip_down.wait_recv()
    edge_row = jnp.concatenate([slip_edge[0, 4 + q : 5 + q, :] for q in range(4)], axis=1)
    window[0:1, :] = jnp.where(has_below, edge_row, 0.0)
    edge_row = jnp.concatenate([slip_edge[1, q : 1 + q, :] for q in range(4)], axis=1)
    window[5:6, :] = jnp.where(has_above, edge_row, 0.0)
    load_near.wait()
    for i in range(2):
        total = jnp.zeros((8, 512), jnp.float32)
        for j in range(3):
            row = window[pl.ds(2 * bi + i + j, 1), :]
            row = jnp.broadcast_to(row, (8, 512)).astype(jnp.bfloat16)
            total = total + lax.dot_general(
                row, near[i, j], (((1,), (1,)), ((), ())), preferred_element_type=jnp.float32
            )
        store_rows(near_own, 4 * i, total[0:1, :])
    near_copy = remote(near_own, near_other, one_send.at[5], one_recv.at[5], other)
    near_copy.start()
    faces(1)

    p_copy.wait_recv()
    r_copy.wait_recv()
    inner = (1 - bi).astype(jnp.float32)
    for plane in range(planes):
        p_lower, r_lower = p_edge[plane, 7:8, :], r_edge[plane, 7:8, :]
        p_upper, r_upper = p_edge[plane, 0:1, :], r_edge[plane, 0:1, :]
        pv[plane, 7:8, :] = p_lower
        rv[plane, 7:8, :] = r_lower + inner * FAR
        pv[plane, HALO + width_y : HALO + width_y + 1, :] = p_upper
        rv[plane, HALO + width_y : HALO + width_y + 1, :] = r_upper + (1.0 - inner) * FAR

    def stencil(y):
        p = [pv[plane, pl.ds(HALO + y, 8), :] for plane in range(planes)]
        r = [rv[plane, pl.ds(HALO + y, 8), :] for plane in range(planes)]
        last = lax.broadcasted_iota(jnp.int32, (8, width_z), 1) == width_z - 1
        between = (p[1] - p[0]) * inverse(r[0] + r[1])
        for plane in range(planes):
            pc, rc = p[plane], r[plane]
            total = between if plane == 0 else -between
            for shift in (1, -1):
                pn = pv.at[plane, pl.ds(y, 24), :][HALO + shift : HALO + shift + 8, :]
                rn = rv.at[plane, pl.ds(y, 24), :][HALO + shift : HALO + shift + 8, :]
                total = total + (pn - pc) * inverse(rn + rc)
            pn = pltpu.roll(pc, width_z - 1, 1)
            rn = pltpu.roll(rc, width_z - 1, 1)
            flux = jnp.where(last, jnp.float32(0.0), (pn - pc) * inverse(rn + rc))
            total = total + flux - pltpu.roll(flux, 1, 1)
            acc[plane, pl.ds(y, 8), :] = total

    def spread_source(step, carry):
        at = pl.ds(pl.multiple_of(step * Z_TILE, Z_TILE), Z_TILE)
        result = lax.dot_general(
            wyx[...], wz[at, :], (((1,), (1,)), ((), ())), preferred_element_type=jnp.float32
        )
        source[0, :, at] = result[:width_y]
        source[1, :, at] = result[width_y:]
        count = width_y // 8 // (width_z // Z_TILE)
        for k in range(count):
            stencil(pl.multiple_of((step * count + k) * 8, 8))
        return carry

    spreads = width_z // Z_TILE
    lax.fori_loop(0, 2, spread_source, 0)
    faces(2)
    lax.fori_loop(2, 3, spread_source, 0)
    faces(3)
    lax.fori_loop(3, spreads, spread_source, 0)

    stores = []
    for part in range(PARTS):
        low = pl.ds(part * rows, rows)
        high = pl.ds(half + part * rows, rows)
        for which, plane, at, flux in (
            (0, 0, low, fsnd.at[0, part]),
            (1, 1, high, fsnd.at[1, part]),
        ):
            value = flux[...].astype(jnp.float32)
            acc[plane, at, :] = acc[plane, at, :] + source[plane, at, :] + value
            copy = pltpu.make_async_copy(
                acc.at[plane, at], rate_hbm.at[plane, at], out_sem.at[which, part]
            )
            copy.start()
            stores.append(copy)

    for copy in last:
        copy.wait()
    column = lanes_row(far_col, 0, 8)
    group = nx * 4
    column = (
        ((column // group) % nz) * (ny * group) + (column // (nz * group)) * group + column % group
    )
    pick[...] = jnp.where(
        lax.broadcasted_iota(jnp.int32, pick.shape, 0) == column, 1.0, 0.0
    ).astype(jnp.bfloat16)
    for copy in z_copies:
        copy.wait_recv()
    moments = gather[...].reshape(512, 128)[:, 0:rank]
    picked = lax.dot_general(
        moments, pick[...], (((0,), (0,)), ((), ())), preferred_element_type=jnp.float32
    )
    ranks = lanes_row(far_rank, 0, 8)
    masked = jnp.where(
        lax.broadcasted_iota(jnp.int32, picked.shape, 0) < ranks, picked, jnp.float32(0.0)
    )
    load_coupling.wait()
    for a in range(rank):
        block[a : a + 1, :] = jnp.sum(
            coupling[a].astype(jnp.float32) * masked, axis=0, keepdims=True
        )
    target = lanes_row(far_row, 0, 8)
    lane = lax.broadcasted_iota(jnp.int32, (rank, 128), 1)
    totals = jnp.zeros((rank, 128), jnp.float32)
    for c in range(4):
        share = jnp.sum(
            jnp.where(target == c, block[...], jnp.float32(0.0)), axis=1, keepdims=True
        )
        totals = totals + jnp.where(lane == c, share, jnp.float32(0.0))
    tot_own[...] = totals
    tot_copy = remote(tot_own, tot_other, one_send.at[6], one_recv.at[6], other)
    tot_copy.start()

    for part in range(PARTS):
        low = pl.ds(part * rows, rows)
        high = pl.ds(half + part * rows, rows)
        for which, plane, at, way, present in (
            (2, 1, low, 0, has_above),
            (3, 0, high, 1, has_below),
        ):
            pl.when(present)(fl_copies[way, part].wait_recv)
            value = frcv[way, part].astype(jnp.float32)
            acc[plane, at, :] = acc[plane, at, :] + source[plane, at, :] - value
            copy = pltpu.make_async_copy(
                acc.at[plane, at], rate_hbm.at[plane, at], out_sem.at[which, part]
            )
            copy.start()
            stores.append(copy)

    tot_copy.wait_recv()
    near_copy.wait_recv()
    fp_copy.wait_recv()
    totals = tot_own[...] + tot_other[...]
    for c in range(4):
        basis = row_basis[:, 512 * c : 512 * (c + 1)].astype(jnp.float32)
        store_rows(
            far16, 4 * c, jnp.sum(basis * totals[:, c : c + 1], axis=0, keepdims=True)
        )
    own, others = near_own[...], near_other[...]
    first = bi == 0
    near16 = jnp.concatenate(
        [jnp.where(first, own, others), jnp.where(first, others, own)], axis=0
    )
    traction = near16 + far16[...]
    effective = stress[...] - (fp_own[...] + fp_other[...])
    rate = slip[...]
    state_rate = jnp.exp(-log_state[...]) - rate
    accel_out[...] = (traction - effective * friction_b[...] * state_rate) / (
        effective * friction_a[...] / rate + 0.5
    )
    state_out[...] = state_rate

    for copy in stores:
        copy.wait()
    for part in range(PARTS):
        for way, there, back in ((0, has_above, has_below), (1, has_below, has_above)):
            pl.when(there)(pr_copies[2 * part + way].wait_send)
            pl.when(back)(fl_copies[way, part].wait_send)
    for copy in xy_copies + z_copies + [slip_up, slip_down, p_copy, r_copy, fp_copy, near_copy, tot_copy]:
        copy.wait_send()


def hand_over(rate_in, accel_in, state_in, rate, accel, state, held, held_two, sem):
    planes, width_y, _ = rate.shape
    part = width_y // 4
    ways = [(accel_in, held_two.at[0], accel), (state_in, held_two.at[1], state)]
    for plane in range(planes):
        for k in range(4):
            at = (plane, pl.ds(part * k, part))
            ways.append((rate_in.at[at], held.at[at], rate.at[at]))
    loads = [
        pltpu.make_async_copy(src, mid, sem.at[0, i]) for i, (src, mid, _) in enumerate(ways)
    ]
    stores = [
        pltpu.make_async_copy(mid, dst, sem.at[1, i]) for i, (_, mid, dst) in enumerate(ways)
    ]
    for load in loads:
        load.start()
    for load, store in zip(loads, stores):
        load.wait()
        store.start()
    for store in stores:
        store.wait()


def shards(
    slip_rate,
    log_state,
    friction_a,
    friction_b,
    normal_stress,
    leak_rate,
    corner,
    fraction,
    near_blocks,
    row_basis,
    col_basis,
    far_row,
    far_col,
    far_rank,
    far_coupling,
    pressure,
    region,
    perm_table,
):
    sizes = tuple(lax.axis_size(name) for name in SLAB)
    ny, nz, nx = sizes
    planes, width_y, width_z = pressure.shape
    cells = slip_rate.shape[0]
    clusters = cells // 512
    slots = far_row.shape[0]
    rank = col_basis.shape[0]
    rows = width_y // 2 // PARTS
    f32, bf16 = jnp.float32, jnp.bfloat16
    vmem = pl.BlockSpec(memory_space=pltpu.VMEM)
    hbm = pl.BlockSpec(memory_space=pl.ANY)
    dma = pltpu.SemaphoreType.DMA

    def cut(x):
        return x.reshape(-1, 128)

    shapes = (
        jax.ShapeDtypeStruct(pressure.shape, f32),
        jax.ShapeDtypeStruct((cells // 128, 128), f32),
        jax.ShapeDtypeStruct((cells // 128, 128), f32),
    )
    results = pl.pallas_call(
        functools.partial(kernel, sizes),
        out_shape=shapes,
        in_specs=[hbm] * 18,
        out_specs=(hbm, vmem, vmem),
        scratch_shapes=[
            *[pltpu.VMEM((cells // 128, 128), f32)] * 6,
            pltpu.VMEM(corner.shape, jnp.int32),
            pltpu.VMEM(fraction.shape, f32),
            pltpu.VMEM(row_basis.shape, bf16),
            pltpu.VMEM(col_basis.shape, bf16),
            *[pltpu.VMEM((slots // 128, 128), jnp.int32)] * 3,
            pltpu.VMEM((1, perm_table.shape[0]), f32),
            pltpu.VMEM((planes, width_y + 2 * HALO, width_z), f32),
            pltpu.VMEM((planes, width_y + 2 * HALO, width_z), f32),
            pltpu.VMEM((planes, width_y, width_z), jnp.int32),
            pltpu.VMEM((planes, width_y, width_z), f32),
            pltpu.VMEM((planes, width_y, width_z), f32),
            pltpu.VMEM((2, PARTS, 2, rows, width_z), bf16),
            pltpu.VMEM((2, PARTS, 2, rows, width_z), bf16),
            pltpu.VMEM((2, PARTS, rows, width_z), bf16),
            pltpu.VMEM((2, PARTS, rows, width_z), bf16),
            pltpu.VMEM((planes, 8, width_z), f32),
            pltpu.VMEM((planes, 8, width_z), f32),
            pltpu.VMEM((width_z, cells), bf16),
            pltpu.VMEM((planes * width_y, cells), bf16),
            pltpu.VMEM((planes * width_y, width_z), bf16),
            pltpu.VMEM(near_blocks.shape, bf16),
            pltpu.VMEM(far_coupling.shape, bf16),
            pltpu.VMEM((ny * nz * nx * clusters, slots), bf16),
            pltpu.VMEM((ny, nx, 8, 128), f32),
            pltpu.VMEM((nz, ny * nx * clusters, 128), bf16),
            pltpu.VMEM((2, 8, 128), f32),
            pltpu.VMEM((8, 512), f32),
            pltpu.VMEM((1, cells), f32),
            pltpu.VMEM((1, cells), f32),
            pltpu.VMEM((cells // 128, 128), f32),
            pltpu.VMEM((cells // 128, 128), f32),
            pltpu.VMEM((8, 128), f32),
            pltpu.VMEM((8, 128), f32),
            pltpu.VMEM((rank, 128), f32),
            pltpu.VMEM((rank, 128), f32),
            pltpu.VMEM((rank, slots), f32),
            pltpu.VMEM((cells // 128, 128), f32),
            dma((24,)),
            dma((ny * nx - 1,)),
            dma((ny * nx - 1,)),
            dma((nz - 1,)),
            dma((nz - 1,)),
            dma((2, PARTS)),
            dma((2, PARTS)),
            dma((2, PARTS)),
            dma((2, PARTS)),
            dma((7,)),
            dma((7,)),
            dma((4, PARTS)),
        ],
        compiler_params=pltpu.CompilerParams(
            collective_id=0, has_side_effects=True, vmem_limit_bytes=60 * 1024 * 1024
        ),
        name="fault_step",
    )(
        cut(slip_rate),
        cut(log_state),
        cut(friction_a),
        cut(friction_b),
        cut(normal_stress),
        cut(leak_rate),
        corner,
        fraction,
        row_basis,
        col_basis,
        cut(far_row),
        cut(far_col),
        cut(far_rank),
        perm_table.reshape(1, -1),
        near_blocks,
        far_coupling,
        pressure,
        region,
    )
    rate, accel, state = pl.pallas_call(
        hand_over,
        out_shape=shapes,
        in_specs=[hbm] * 3,
        out_specs=(hbm,) * 3,
        scratch_shapes=[
            pltpu.VMEM(pressure.shape, f32),
            pltpu.VMEM((2, cells // 128, 128), f32),
            dma((2, 10)),
        ],
        compiler_params=pltpu.CompilerParams(vmem_limit_bytes=60 * 1024 * 1024),
        name="hand_over",
    )(*results)
    return accel.reshape(cells), state.reshape(cells), rate


def solution(mesh):
    torus = Mesh(
        mesh.devices.reshape(4, 8, 4, mesh.shape["blk"]), ("slab_0", "slab_1", "slab_2", "blk")
    )
    placed = (
        P(SLAB),
        P(SLAB),
        P(SLAB),
        P(SLAB),
        P(SLAB),
        P(SLAB),
        P(None, SLAB),
        P(None, SLAB),
        P(SLAB_BLK, None, None, None),
        P(None, SLAB),
        P(None, SLAB),
        P(SLAB_BLK),
        P(SLAB_BLK),
        P(SLAB_BLK),
        P(None, None, SLAB_BLK),
        P(SLAB, "blk", None),
        P(SLAB, "blk", None),
        P(),
    )
    return jax.shard_map(
        shards,
        mesh=torus,
        in_specs=placed,
        out_specs=(P(SLAB), P(SLAB), P(SLAB, "blk", None)),
        check_vma=False,
    )
```

```python
import functools

import jax
import jax.numpy as jnp
from jax import lax
from jax.experimental import pallas as pl
from jax.experimental.pallas import tpu as pltpu
from jax.sharding import Mesh
from jax.sharding import PartitionSpec as P

SLAB = ("slab_0", "slab_1", "slab_2")
SLAB_BLK = ("slab_0", "slab_1", "slab_2", "blk")
MESH = pl.DeviceIdType.MESH

PARTS = 4
F_TILE = 512
Z_TILE = 256
HALO = 8
FAR = 1e30


def lanes_row(ref, first, count):
    return jnp.concatenate([ref[first + q : first + q + 1, :] for q in range(count)], axis=1)


def store_rows(ref, first, row):
    for q in range(row.shape[1] // 128):
        ref[first + q : first + q + 1, :] = row[:, 128 * q : 128 * (q + 1)]


def inverse(x):
    return pl.reciprocal(x, approx=True)


def kernel(
    sizes,
    slip_hbm,
    log_state_hbm,
    friction_a_hbm,
    friction_b_hbm,
    stress_hbm,
    leak_hbm,
    corner_hbm,
    fraction_hbm,
    row_basis_hbm,
    col_basis_hbm,
    far_row_hbm,
    far_col_hbm,
    far_rank_hbm,
    table_hbm,
    near_hbm,
    coupling_hbm,
    p_hbm,
    region_hbm,
    rate_hbm,
    accel_out,
    state_out,
    slip,
    log_state,
    friction_a,
    friction_b,
    stress,
    leak,
    corner,
    fraction,
    row_basis,
    col_basis,
    far_row,
    far_col,
    far_rank,
    table,
    pv,
    rv,
    region,
    acc,
    source,
    snd,
    rcv,
    fsnd,
    frcv,
    p_edge,
    r_edge,
    wz,
    wyx,
    p_low,
    near,
    coupling,
    pick,
    gather_x,
    gather,
    slip_edge,
    window,
    flow_row,
    fp_row,
    fp_own,
    fp_other,
    near_own,
    near_other,
    tot_own,
    tot_other,
    block,
    far16,
    load_sem,
    x_send,
    x_recv,
    z_send,
    z_recv,
    y_send,
    y_recv,
    pr_send,
    pr_recv,
    fl_send,
    fl_recv,
    one_send,
    one_recv,
    out_sem,
):
    ny, nz, nx = sizes
    slabs = ny * nz * nx
    planes, width_y, width_z = region.shape
    half = width_y // 2
    rows = half // PARTS
    rank = col_basis.shape[0]
    cells = corner.shape[1]
    yi, zi, xi = (lax.axis_index(name) for name in SLAB)
    bi = lax.axis_index("blk")
    slab = (yi * nz + zi) * nx + xi

    def chip_of(index):
        return (
            lax.div(index, nz * nx),
            lax.rem(lax.div(index, nx), nz),
            lax.rem(index, nx),
            bi,
        )

    above = chip_of(lax.rem(slab + 1, slabs))
    below = chip_of(lax.rem(slab + slabs - 1, slabs))
    other = (yi, zi, xi, 1 - bi)
    x_peers = [(yi, zi, lax.rem(xi + d, nx), bi) for d in range(1, nx)]
    y_peers = [(lax.rem(yi + d, ny), zi, xi, bi) for d in range(1, ny)]
    z_peers = [(yi, lax.rem(zi + d, nz), xi, bi) for d in range(1, nz)]
    has_below, has_above = slab > 0, slab < slabs - 1

    barrier = pltpu.get_barrier_semaphore()
    peers = [above, below, other] + x_peers + z_peers + y_peers
    for peer in peers:
        pl.semaphore_signal(barrier, inc=1, device_id=peer, device_id_type=MESH)

    def remote(src, dst, send, recv, device):
        return pltpu.make_async_remote_copy(
            src_ref=src,
            dst_ref=dst,
            send_sem=send,
            recv_sem=recv,
            device_id=device,
            device_id_type=MESH,
        )

    def quarter(plane, part, sem):
        at = pl.ds(part * half, half)
        to = pl.ds(HALO + part * half, half)
        return (
            pltpu.make_async_copy(
                region_hbm.at[plane, at], region.at[plane, at], load_sem.at[sem]
            ),
            pltpu.make_async_copy(p_hbm.at[plane, at], pv.at[plane, to], load_sem.at[sem + 1]),
        )

    first_up, first_down = quarter(1, 0, 0), quarter(0, 1, 2)
    later = quarter(0, 0, 4) + quarter(1, 1, 6)
    small = [
        pltpu.make_async_copy(src, dst, load_sem.at[10 + i])
        for i, (src, dst) in enumerate(
            (
                (slip_hbm, slip),
                (col_basis_hbm, col_basis),
                (table_hbm, table),
                (leak_hbm, leak),
                (corner_hbm, corner),
                (fraction_hbm, fraction),
                (far_col_hbm, far_col),
                (far_rank_hbm, far_rank),
                (far_row_hbm, far_row),
                (row_basis_hbm, row_basis),
                (stress_hbm, stress),
                (log_state_hbm, log_state),
                (friction_a_hbm, friction_a),
                (friction_b_hbm, friction_b),
            )
        )
    ]
    load_near = pltpu.make_async_copy(near_hbm, near, load_sem.at[8])
    load_coupling = pltpu.make_async_copy(coupling_hbm, coupling, load_sem.at[9])
    ahead = small[:4]
    behind = small[4:6]
    last = small[6:]
    for copy in ahead[:3] + list(first_up + first_down) + ahead[3:] + behind + list(later):
        copy.start()
    for copy in ahead:
        copy.wait()

    for c in range(4):
        window[1 + c : 2 + c, :] = lanes_row(slip, 4 * c, 4)
    slip_row = jnp.concatenate([window[1 + c : 2 + c, :] for c in range(4)], axis=1)
    spread = jnp.broadcast_to(slip_row, (8, cells))
    lane = lax.broadcasted_iota(jnp.int32, (8, cells), 1)
    sub = lax.broadcasted_iota(jnp.int32, (8, cells), 0)
    spread = jnp.where(
        (lane >= sub * 512) & (lane < sub * 512 + 512), spread, jnp.float32(0.0)
    ).astype(jnp.bfloat16)
    moments = lax.dot_general(
        spread, col_basis[...], (((1,), (1,)), ((), ())), preferred_element_type=jnp.float32
    )
    gather_x[xi] = jnp.zeros((8, 128), jnp.float32)
    gather_x[xi, :, 0:rank] = moments
    for c in range(16):
        flow_row[:, 128 * c : 128 * (c + 1)] = leak[c : c + 1, :] * slip[c : c + 1, :]

    pl.semaphore_wait(barrier, len(peers))

    x_copies = [
        remote(gather_x.at[xi], gather_x.at[xi], x_send.at[d], x_recv.at[d], peer)
        for d, peer in enumerate(x_peers)
    ]
    for copy in x_copies:
        copy.start()
    slip_up = remote(slip.at[8:16], slip_edge.at[0], one_send.at[0], one_recv.at[0], above)
    slip_down = remote(slip.at[0:8], slip_edge.at[1], one_send.at[1], one_recv.at[1], below)
    slip_up.start()
    slip_down.start()

    halves = jnp.concatenate([0.5 / table[...], jnp.zeros((1, 128 - table.shape[1]), jnp.float32)], axis=1)

    def look_up(plane, start, count):
        chosen = region[plane, pl.ds(start, count), :]
        entries = jnp.broadcast_to(halves, (count, 128))
        r = jnp.concatenate(
            [
                jnp.take_along_axis(
                    entries,
                    chosen[:, 128 * j : 128 * (j + 1)],
                    axis=1,
                    mode="promise_in_bounds",
                )
                for j in range(width_z // 128)
            ],
            axis=1,
        )
        p = pv[plane, pl.ds(HALO + start, count), :].astype(jnp.bfloat16)
        rv[plane, pl.ds(HALO + start, count), :] = r
        p_low[pl.ds(plane * width_y + start, count), :] = p
        return p, r.astype(jnp.bfloat16)

    pr_copies = []
    for part in range(PARTS):
        for way, plane, offset, device, loads, present in (
            (0, 1, 0, above, first_up, has_above),
            (1, 0, half, below, first_down, has_below),
        ):
            if part == 0:
                for copy in loads:
                    copy.wait()
            p, r = look_up(plane, offset + part * rows, rows)
            snd[way, part, 0] = p
            snd[way, part, 1] = r
            copy = remote(
                snd.at[way, part],
                rcv.at[way, part],
                pr_send.at[way, part],
                pr_recv.at[way, part],
                device,
            )
            if part < PARTS - 1:
                pl.when(present)(copy.start)
            pr_copies.append(copy)

    for copy in [load_near, load_coupling] + last:
        copy.start()
    for copy in later + tuple(behind):
        copy.wait()

    def rest(step, carry):
        start = pl.multiple_of(step * rows, rows)
        look_up(0, start, rows)
        look_up(1, start + half, rows)
        return carry

    lax.fori_loop(0, PARTS, rest, 0)

    edge = pl.multiple_of(HALO + (1 - bi) * (width_y - 8), 8)
    p_copy = remote(
        pv.at[:, pl.ds(edge, 8), :], p_edge, one_send.at[2], one_recv.at[2], other
    )
    r_copy = remote(
        rv.at[:, pl.ds(edge, 8), :], r_edge, one_send.at[3], one_recv.at[3], other
    )
    p_copy.start()
    r_copy.start()

    y_start = bi * width_y

    def sample(step, carry):
        at = pl.ds(pl.multiple_of(step * F_TILE, F_TILE), F_TILE)
        z = corner[2:3, at]
        fz = fraction[2:3, at]
        iota = lax.broadcasted_iota(jnp.int16, (width_z, F_TILE), 0)
        z = jnp.broadcast_to(z, (16, F_TILE)).astype(jnp.int16)[0:1]
        weight = jnp.where(
            iota == z,
            (1.0 - fz).astype(jnp.bfloat16),
            jnp.where(iota == z + 1, fz.astype(jnp.bfloat16), jnp.bfloat16(0.0)),
        )
        wz[:, at] = weight
        along_z = jnp.dot(p_low[...], weight, preferred_element_type=jnp.float32)
        y = corner[1:2, at] - y_start
        fy = fraction[1:2, at]
        fx = fraction[0:1, at]
        flow = flow_row[:, at]
        iota = lax.broadcasted_iota(jnp.int32, (width_y, F_TILE), 0)
        weight_y = jnp.where(iota == y, 1.0 - fy, jnp.where(iota == y + 1, fy, jnp.float32(0.0)))
        low = jnp.sum(along_z[:width_y] * weight_y, axis=0, keepdims=True)
        high = jnp.sum(along_z[width_y:] * weight_y, axis=0, keepdims=True)
        fp_row[:, at] = (1.0 - fx) * low + fx * high
        wyx[0:width_y, at] = (weight_y * ((1.0 - fx) * flow)).astype(jnp.bfloat16)
        wyx[width_y:, at] = (weight_y * (fx * flow)).astype(jnp.bfloat16)
        return carry

    steps = cells // F_TILE
    lax.fori_loop(0, 1, sample, 0)
    pl.when(has_above)(pr_copies[2 * PARTS - 2].start)
    pl.when(has_below)(pr_copies[2 * PARTS - 1].start)

    for copy in x_copies:
        copy.wait_recv()
    mine = jnp.concatenate(
        [gather_x[i, 0:4, :] for i in range(nx)], axis=0
    )
    gather[yi, zi] = mine.astype(jnp.bfloat16)
    z_copies = [
        remote(gather.at[yi, zi], gather.at[yi, zi], z_send.at[d], z_recv.at[d], peer)
        for d, peer in enumerate(z_peers)
    ]
    for copy in z_copies:
        copy.start()

    fl_copies = {}

    def faces(part):
        for way, plane, offset, device, present in (
            (0, 0, 0, below, has_below),
            (1, 1, half, above, has_above),
        ):
            copy = remote(
                fsnd.at[way, part],
                frcv.at[way, part],
                fl_send.at[way, part],
                fl_recv.at[way, part],
                device,
            )
            fl_copies[way, part] = copy

            @pl.when(present)
            def _(way=way, plane=plane, offset=offset, copy=copy):
                pr_copies[2 * part + way].wait_recv()
                at = pl.ds(HALO + offset + part * rows, rows)
                p_in = rcv[way, part, 0].astype(jnp.float32)
                r_in = rcv[way, part, 1].astype(jnp.float32)
                drop = p_in - pv[plane, at, :]
                flux = drop * inverse(rv[plane, at, :] + r_in)
                fsnd[way, part] = flux.astype(jnp.bfloat16)
                copy.start()

            @pl.when(jnp.logical_not(present))
            def _(way=way):
                fsnd[way, part] = jnp.zeros((rows, width_z), jnp.bfloat16)
                frcv[1 - way, part] = jnp.zeros((rows, width_z), jnp.bfloat16)

    lax.fori_loop(1, 3, sample, 0)
    faces(0)
    lax.fori_loop(3, steps, sample, 0)
    for c in range(16):
        fp_own[c : c + 1, :] = fp_row[:, 128 * c : 128 * (c + 1)]
    fp_copy = remote(fp_own, fp_other, one_send.at[4], one_recv.at[4], other)
    fp_copy.start()

    for copy in z_copies:
        copy.wait_recv()
    y_copies = [
        remote(gather.at[yi], gather.at[yi], y_send.at[d], y_recv.at[d], peer)
        for d, peer in enumerate(y_peers)
    ]
    for copy in y_copies:
        copy.start()

    slip_up.wait_recv()
    slip_down.wait_recv()
    edge_row = jnp.concatenate([slip_edge[0, 4 + q : 5 + q, :] for q in range(4)], axis=1)
    window[0:1, :] = jnp.where(has_below, edge_row, 0.0)
    edge_row = jnp.concatenate([slip_edge[1, q : 1 + q, :] for q in range(4)], axis=1)
    window[5:6, :] = jnp.where(has_above, edge_row, 0.0)
    load_near.wait()
    for i in range(2):
        total = jnp.zeros((8, 512), jnp.float32)
        for j in range(3):
            row = window[pl.ds(2 * bi + i + j, 1), :]
            row = jnp.broadcast_to(row, (8, 512)).astype(jnp.bfloat16)
            total = total + lax.dot_general(
                row, near[i, j], (((1,), (1,)), ((), ())), preferred_element_type=jnp.float32
            )
        store_rows(near_own, 4 * i, total[0:1, :])
    near_copy = remote(near_own, near_other, one_send.at[5], one_recv.at[5], other)
    near_copy.start()
    faces(1)

    p_copy.wait_recv()
    r_copy.wait_recv()
    inner = (1 - bi).astype(jnp.float32)
    for plane in range(planes):
        p_lower, r_lower = p_edge[plane, 7:8, :], r_edge[plane, 7:8, :]
        p_upper, r_upper = p_edge[plane, 0:1, :], r_edge[plane, 0:1, :]
        pv[plane, 7:8, :] = p_lower
        rv[plane, 7:8, :] = r_lower + inner * FAR
        pv[plane, HALO + width_y : HALO + width_y + 1, :] = p_upper
        rv[plane, HALO + width_y : HALO + width_y + 1, :] = r_upper + (1.0 - inner) * FAR

    def stencil(y):
        p = [pv[plane, pl.ds(HALO + y, 8), :] for plane in range(planes)]
        r = [rv[plane, pl.ds(HALO + y, 8), :] for plane in range(planes)]
        last = lax.broadcasted_iota(jnp.int32, (8, width_z), 1) == width_z - 1
        between = (p[1] - p[0]) * inverse(r[0] + r[1])
        for plane in range(planes):
            pc, rc = p[plane], r[plane]
            total = between if plane == 0 else -between
            for shift in (1, -1):
                pn = pv.at[plane, pl.ds(y, 24), :][HALO + shift : HALO + shift + 8, :]
                rn = rv.at[plane, pl.ds(y, 24), :][HALO + shift : HALO + shift + 8, :]
                total = total + (pn - pc) * inverse(rn + rc)
            pn = pltpu.roll(pc, width_z - 1, 1)
            rn = pltpu.roll(rc, width_z - 1, 1)
            flux = jnp.where(last, jnp.float32(0.0), (pn - pc) * inverse(rn + rc))
            total = total + flux - pltpu.roll(flux, 1, 1)
            acc[plane, pl.ds(y, 8), :] = total

    def spread_source(step, carry):
        at = pl.ds(pl.multiple_of(step * Z_TILE, Z_TILE), Z_TILE)
        result = lax.dot_general(
            wyx[...], wz[at, :], (((1,), (1,)), ((), ())), preferred_element_type=jnp.float32
        )
        source[0, :, at] = result[:width_y]
        source[1, :, at] = result[width_y:]
        count = width_y // 8 // (width_z // Z_TILE)
        for k in range(count):
            stencil(pl.multiple_of((step * count + k) * 8, 8))
        return carry

    spreads = width_z // Z_TILE
    lax.fori_loop(0, 2, spread_source, 0)
    faces(2)
    lax.fori_loop(2, 3, spread_source, 0)
    faces(3)
    for copy in last:
        copy.wait()
    column = lanes_row(far_col, 0, 8)
    pick[...] = jnp.where(
        lax.broadcasted_iota(jnp.int32, pick.shape, 0) == column, 1.0, 0.0
    ).astype(jnp.bfloat16)
    for copy in y_copies:
        copy.wait_recv()
    moments = gather[...].reshape(512, 128)[:, 0:rank]
    picked = lax.dot_general(
        moments, pick[...], (((0,), (0,)), ((), ())), preferred_element_type=jnp.float32
    )
    ranks = lanes_row(far_rank, 0, 8)
    masked = jnp.where(
        lax.broadcasted_iota(jnp.int32, picked.shape, 0) < ranks, picked, jnp.float32(0.0)
    )
    load_coupling.wait()
    for a in range(rank):
        block[a : a + 1, :] = jnp.sum(
            coupling[a].astype(jnp.float32) * masked, axis=0, keepdims=True
        )
    target = lanes_row(far_row, 0, 8)
    lane = lax.broadcasted_iota(jnp.int32, (rank, 128), 1)
    totals = jnp.zeros((rank, 128), jnp.float32)
    for c in range(4):
        share = jnp.sum(
            jnp.where(target == c, block[...], jnp.float32(0.0)), axis=1, keepdims=True
        )
        totals = totals + jnp.where(lane == c, share, jnp.float32(0.0))
    tot_own[...] = totals
    tot_copy = remote(tot_own, tot_other, one_send.at[6], one_recv.at[6], other)
    tot_copy.start()

    lax.fori_loop(3, spreads, spread_source, 0)

    stores = []
    for part in range(PARTS):
        low = pl.ds(part * rows, rows)
        high = pl.ds(half + part * rows, rows)
        for which, plane, at, flux in (
            (0, 0, low, fsnd.at[0, part]),
            (1, 1, high, fsnd.at[1, part]),
        ):
            value = flux[...].astype(jnp.float32)
            acc[plane, at, :] = acc[plane, at, :] + source[plane, at, :] + value
            copy = pltpu.make_async_copy(
                acc.at[plane, at], rate_hbm.at[plane, at], out_sem.at[which, part]
            )
            copy.start()
            stores.append(copy)

    for part in range(PARTS):
        low = pl.ds(part * rows, rows)
        high = pl.ds(half + part * rows, rows)
        for which, plane, at, way, present in (
            (2, 1, low, 0, has_above),
            (3, 0, high, 1, has_below),
        ):
            pl.when(present)(fl_copies[way, part].wait_recv)
            value = frcv[way, part].astype(jnp.float32)
            acc[plane, at, :] = acc[plane, at, :] + source[plane, at, :] - value
            copy = pltpu.make_async_copy(
                acc.at[plane, at], rate_hbm.at[plane, at], out_sem.at[which, part]
            )
            copy.start()
            stores.append(copy)

    tot_copy.wait_recv()
    near_copy.wait_recv()
    fp_copy.wait_recv()
    totals = tot_own[...] + tot_other[...]
    for c in range(4):
        basis = row_basis[:, 512 * c : 512 * (c + 1)].astype(jnp.float32)
        store_rows(
            far16, 4 * c, jnp.sum(basis * totals[:, c : c + 1], axis=0, keepdims=True)
        )
    own, others = near_own[...], near_other[...]
    first = bi == 0
    near16 = jnp.concatenate(
        [jnp.where(first, own, others), jnp.where(first, others, own)], axis=0
    )
    traction = near16 + far16[...]
    effective = stress[...] - (fp_own[...] + fp_other[...])
    rate = slip[...]
    state_rate = jnp.exp(-log_state[...]) - rate
    accel_out[...] = (traction - effective * friction_b[...] * state_rate) / (
        effective * friction_a[...] / rate + 0.5
    )
    state_out[...] = state_rate

    for copy in stores:
        copy.wait()
    for part in range(PARTS):
        for way, there, back in ((0, has_above, has_below), (1, has_below, has_above)):
            pl.when(there)(pr_copies[2 * part + way].wait_send)
            pl.when(back)(fl_copies[way, part].wait_send)
    for copy in x_copies + z_copies + y_copies + [slip_up, slip_down, p_copy, r_copy, fp_copy, near_copy, tot_copy]:
        copy.wait_send()


def hand_over(rate_in, accel_in, state_in, rate, accel, state, held, held_two, sem):
    planes, width_y, _ = rate.shape
    part = width_y // 4
    ways = [(accel_in, held_two.at[0], accel), (state_in, held_two.at[1], state)]
    for plane in range(planes):
        for k in range(4):
            at = (plane, pl.ds(part * k, part))
            ways.append((rate_in.at[at], held.at[at], rate.at[at]))
    loads = [
        pltpu.make_async_copy(src, mid, sem.at[0, i]) for i, (src, mid, _) in enumerate(ways)
    ]
    stores = [
        pltpu.make_async_copy(mid, dst, sem.at[1, i]) for i, (_, mid, dst) in enumerate(ways)
    ]
    for load in loads:
        load.start()
    for load, store in zip(loads, stores):
        load.wait()
        store.start()
    for store in stores:
        store.wait()


def shards(
    slip_rate,
    log_state,
    friction_a,
    friction_b,
    normal_stress,
    leak_rate,
    corner,
    fraction,
    near_blocks,
    row_basis,
    col_basis,
    far_row,
    far_col,
    far_rank,
    far_coupling,
    pressure,
    region,
    perm_table,
):
    sizes = tuple(lax.axis_size(name) for name in SLAB)
    ny, nz, nx = sizes
    planes, width_y, width_z = pressure.shape
    cells = slip_rate.shape[0]
    clusters = cells // 512
    slots = far_row.shape[0]
    rank = col_basis.shape[0]
    rows = width_y // 2 // PARTS
    f32, bf16 = jnp.float32, jnp.bfloat16
    vmem = pl.BlockSpec(memory_space=pltpu.VMEM)
    hbm = pl.BlockSpec(memory_space=pl.ANY)
    dma = pltpu.SemaphoreType.DMA

    def cut(x):
        return x.reshape(-1, 128)

    shapes = (
        jax.ShapeDtypeStruct(pressure.shape, f32),
        jax.ShapeDtypeStruct((cells // 128, 128), f32),
        jax.ShapeDtypeStruct((cells // 128, 128), f32),
    )
    results = pl.pallas_call(
        functools.partial(kernel, sizes),
        out_shape=shapes,
        in_specs=[hbm] * 18,
        out_specs=(hbm, vmem, vmem),
        scratch_shapes=[
            *[pltpu.VMEM((cells // 128, 128), f32)] * 6,
            pltpu.VMEM(corner.shape, jnp.int32),
            pltpu.VMEM(fraction.shape, f32),
            pltpu.VMEM(row_basis.shape, bf16),
            pltpu.VMEM(col_basis.shape, bf16),
            *[pltpu.VMEM((slots // 128, 128), jnp.int32)] * 3,
            pltpu.VMEM((1, perm_table.shape[0]), f32),
            pltpu.VMEM((planes, width_y + 2 * HALO, width_z), f32),
            pltpu.VMEM((planes, width_y + 2 * HALO, width_z), f32),
            pltpu.VMEM((planes, width_y, width_z), jnp.int32),
            pltpu.VMEM((planes, width_y, width_z), f32),
            pltpu.VMEM((planes, width_y, width_z), f32),
            pltpu.VMEM((2, PARTS, 2, rows, width_z), bf16),
            pltpu.VMEM((2, PARTS, 2, rows, width_z), bf16),
            pltpu.VMEM((2, PARTS, rows, width_z), bf16),
            pltpu.VMEM((2, PARTS, rows, width_z), bf16),
            pltpu.VMEM((planes, 8, width_z), f32),
            pltpu.VMEM((planes, 8, width_z), f32),
            pltpu.VMEM((width_z, cells), bf16),
            pltpu.VMEM((planes * width_y, cells), bf16),
            pltpu.VMEM((planes * width_y, width_z), bf16),
            pltpu.VMEM(near_blocks.shape, bf16),
            pltpu.VMEM(far_coupling.shape, bf16),
            pltpu.VMEM((ny * nz * nx * clusters, slots), bf16),
            pltpu.VMEM((nx, 8, 128), f32),
            pltpu.VMEM((ny, nz, nx * clusters, 128), bf16),
            pltpu.VMEM((2, 8, 128), f32),
            pltpu.VMEM((8, 512), f32),
            pltpu.VMEM((1, cells), f32),
            pltpu.VMEM((1, cells), f32),
            pltpu.VMEM((cells // 128, 128), f32),
            pltpu.VMEM((cells // 128, 128), f32),
            pltpu.VMEM((8, 128), f32),
            pltpu.VMEM((8, 128), f32),
            pltpu.VMEM((rank, 128), f32),
            pltpu.VMEM((rank, 128), f32),
            pltpu.VMEM((rank, slots), f32),
            pltpu.VMEM((cells // 128, 128), f32),
            dma((24,)),
            dma((nx - 1,)),
            dma((nx - 1,)),
            dma((nz - 1,)),
            dma((nz - 1,)),
            dma((ny - 1,)),
            dma((ny - 1,)),
            dma((2, PARTS)),
            dma((2, PARTS)),
            dma((2, PARTS)),
            dma((2, PARTS)),
            dma((7,)),
            dma((7,)),
            dma((4, PARTS)),
        ],
        compiler_params=pltpu.CompilerParams(
            collective_id=0, has_side_effects=True, vmem_limit_bytes=60 * 1024 * 1024
        ),
        name="fault_step",
    )(
        cut(slip_rate),
        cut(log_state),
        cut(friction_a),
        cut(friction_b),
        cut(normal_stress),
        cut(leak_rate),
        corner,
        fraction,
        row_basis,
        col_basis,
        cut(far_row),
        cut(far_col),
        cut(far_rank),
        perm_table.reshape(1, -1),
        near_blocks,
        far_coupling,
        pressure,
        region,
    )
    rate, accel, state = pl.pallas_call(
        hand_over,
        out_shape=shapes,
        in_specs=[hbm] * 3,
        out_specs=(hbm,) * 3,
        scratch_shapes=[
            pltpu.VMEM(pressure.shape, f32),
            pltpu.VMEM((2, cells // 128, 128), f32),
            dma((2, 10)),
        ],
        compiler_params=pltpu.CompilerParams(vmem_limit_bytes=60 * 1024 * 1024),
        name="hand_over",
    )(*results)
    return accel.reshape(cells), state.reshape(cells), rate


def solution(mesh):
    torus = Mesh(
        mesh.devices.reshape(4, 8, 4, mesh.shape["blk"]), ("slab_0", "slab_1", "slab_2", "blk")
    )
    placed = (
        P(SLAB),
        P(SLAB),
        P(SLAB),
        P(SLAB),
        P(SLAB),
        P(SLAB),
        P(None, SLAB),
        P(None, SLAB),
        P(SLAB_BLK, None, None, None),
        P(None, SLAB),
        P(None, SLAB),
        P(SLAB_BLK),
        P(SLAB_BLK),
        P(SLAB_BLK),
        P(None, None, SLAB_BLK),
        P(SLAB, "blk", None),
        P(SLAB, "blk", None),
        P(),
    )
    return jax.shard_map(
        shards,
        mesh=torus,
        in_specs=placed,
        out_specs=(P(SLAB), P(SLAB), P(SLAB, "blk", None)),
        check_vma=False,
    )
```

```python
import functools

import jax
import jax.numpy as jnp
from jax import lax
from jax.experimental import pallas as pl
from jax.experimental.pallas import tpu as pltpu
from jax.sharding import Mesh
from jax.sharding import PartitionSpec as P

SLAB = ("slab_0", "slab_1", "slab_2")
SLAB_BLK = ("slab_0", "slab_1", "slab_2", "blk")
MESH = pl.DeviceIdType.MESH

PARTS = 4
F_TILE = 512
Z_TILE = 256
HALO = 8
FAR = 1e30


def lanes_row(ref, first, count):
    return jnp.concatenate([ref[first + q : first + q + 1, :] for q in range(count)], axis=1)


def store_rows(ref, first, row):
    for q in range(row.shape[1] // 128):
        ref[first + q : first + q + 1, :] = row[:, 128 * q : 128 * (q + 1)]


def inverse(x):
    return pl.reciprocal(x, approx=True)


def kernel(
    sizes,
    slip_hbm,
    log_state_hbm,
    friction_a_hbm,
    friction_b_hbm,
    stress_hbm,
    leak_hbm,
    corner_hbm,
    fraction_hbm,
    row_basis_hbm,
    col_basis_hbm,
    far_row_hbm,
    far_col_hbm,
    far_rank_hbm,
    table_hbm,
    near_hbm,
    coupling_hbm,
    p_hbm,
    region_hbm,
    rate_hbm,
    accel_out,
    state_out,
    slip,
    log_state,
    friction_a,
    friction_b,
    stress,
    leak,
    corner,
    fraction,
    row_basis,
    col_basis,
    far_row,
    far_col,
    far_rank,
    table,
    pv,
    rv,
    region,
    acc,
    source,
    snd,
    rcv,
    fsnd,
    frcv,
    p_edge,
    r_edge,
    wz,
    wyx,
    p_low,
    near,
    coupling,
    pick,
    gather_x,
    gather,
    slip_edge,
    window,
    flow_row,
    fp_row,
    fp_own,
    fp_other,
    near_own,
    near_other,
    tot_own,
    tot_other,
    block,
    far16,
    load_sem,
    x_send,
    x_recv,
    z_send,
    z_recv,
    y_send,
    y_recv,
    pr_send,
    pr_recv,
    fl_send,
    fl_recv,
    one_send,
    one_recv,
    out_sem,
):
    ny, nz, nx = sizes
    slabs = ny * nz * nx
    planes, width_y, width_z = region.shape
    half = width_y // 2
    rows = half // PARTS
    rank = col_basis.shape[0]
    cells = corner.shape[1]
    yi, zi, xi = (lax.axis_index(name) for name in SLAB)
    bi = lax.axis_index("blk")
    slab = (yi * nz + zi) * nx + xi

    def chip_of(index):
        return (
            lax.div(index, nz * nx),
            lax.rem(lax.div(index, nx), nz),
            lax.rem(index, nx),
            bi,
        )

    above = chip_of(lax.rem(slab + 1, slabs))
    below = chip_of(lax.rem(slab + slabs - 1, slabs))
    other = (yi, zi, xi, 1 - bi)
    x_peers = [(yi, zi, lax.rem(xi + d, nx), bi) for d in range(1, nx)]
    z_peers = [(yi, lax.rem(zi + d, nz), xi, bi) for d in range(1, nz)]
    y_peers = [(lax.rem(yi + d, ny), zi, xi, bi) for d in range(1, ny)]

    barrier = pltpu.get_barrier_semaphore()
    peers = [above, below, other] + x_peers + z_peers + y_peers
    for peer in peers:
        pl.semaphore_signal(barrier, inc=1, device_id=peer, device_id_type=MESH)

    def remote(src, dst, send, recv, device):
        return pltpu.make_async_remote_copy(
            src_ref=src,
            dst_ref=dst,
            send_sem=send,
            recv_sem=recv,
            device_id=device,
            device_id_type=MESH,
        )

    def quarter(plane, part, sem):
        at = pl.ds(part * half, half)
        to = pl.ds(HALO + part * half, half)
        return (
            pltpu.make_async_copy(
                region_hbm.at[plane, at], region.at[plane, at], load_sem.at[sem]
            ),
            pltpu.make_async_copy(p_hbm.at[plane, at], pv.at[plane, to], load_sem.at[sem + 1]),
        )

    first_up, first_down = quarter(1, 0, 0), quarter(0, 1, 2)
    later = quarter(0, 0, 4) + quarter(1, 1, 6)
    small = [
        pltpu.make_async_copy(src, dst, load_sem.at[10 + i])
        for i, (src, dst) in enumerate(
            (
                (slip_hbm, slip),
                (col_basis_hbm, col_basis),
                (table_hbm, table),
                (leak_hbm, leak),
                (corner_hbm, corner),
                (fraction_hbm, fraction),
                (far_col_hbm, far_col),
                (far_rank_hbm, far_rank),
                (far_row_hbm, far_row),
                (row_basis_hbm, row_basis),
                (stress_hbm, stress),
                (log_state_hbm, log_state),
                (friction_a_hbm, friction_a),
                (friction_b_hbm, friction_b),
            )
        )
    ]
    load_near = pltpu.make_async_copy(near_hbm, near, load_sem.at[8])
    load_coupling = pltpu.make_async_copy(coupling_hbm, coupling, load_sem.at[9])
    ahead = small[:4]
    behind = small[4:6]
    last = small[6:]
    for copy in ahead[:3] + list(first_up + first_down) + ahead[3:] + behind + list(later):
        copy.start()
    for copy in [load_near, load_coupling] + last:
        copy.start()
    for copy in ahead:
        copy.wait()

    for c in range(4):
        window[1 + c : 2 + c, :] = lanes_row(slip, 4 * c, 4)
    slip_row = jnp.concatenate([window[1 + c : 2 + c, :] for c in range(4)], axis=1)
    spread = jnp.broadcast_to(slip_row, (8, cells))
    lane = lax.broadcasted_iota(jnp.int32, (8, cells), 1)
    sub = lax.broadcasted_iota(jnp.int32, (8, cells), 0)
    spread = jnp.where(
        (lane >= sub * 512) & (lane < sub * 512 + 512), spread, jnp.float32(0.0)
    ).astype(jnp.bfloat16)
    moments = lax.dot_general(
        spread, col_basis[...], (((1,), (1,)), ((), ())), preferred_element_type=jnp.float32
    )
    gather_x[xi] = jnp.zeros((8, 128), jnp.float32)
    gather_x[xi, :, 0:rank] = moments
    for c in range(16):
        flow_row[:, 128 * c : 128 * (c + 1)] = leak[c : c + 1, :] * slip[c : c + 1, :]

    pl.semaphore_wait(barrier, len(peers))

    x_copies = [
        remote(gather_x.at[xi], gather_x.at[xi], x_send.at[d], x_recv.at[d], peer)
        for d, peer in enumerate(x_peers)
    ]
    for copy in x_copies:
        copy.start()
    slip_up = remote(slip.at[8:16], slip_edge.at[0], one_send.at[0], one_recv.at[0], above)
    slip_down = remote(slip.at[0:8], slip_edge.at[1], one_send.at[1], one_recv.at[1], below)
    slip_up.start()
    slip_down.start()

    halves = jnp.concatenate([0.5 / table[...], jnp.zeros((1, 128 - table.shape[1]), jnp.float32)], axis=1)

    def look_up(plane, start, count):
        chosen = region[plane, pl.ds(start, count), :]
        entries = jnp.broadcast_to(halves, (count, 128))
        r = jnp.concatenate(
            [
                jnp.take_along_axis(
                    entries,
                    chosen[:, 128 * j : 128 * (j + 1)],
                    axis=1,
                    mode="promise_in_bounds",
                )
                for j in range(width_z // 128)
            ],
            axis=1,
        )
        p = pv[plane, pl.ds(HALO + start, count), :].astype(jnp.bfloat16)
        rv[plane, pl.ds(HALO + start, count), :] = r
        p_low[pl.ds(plane * width_y + start, count), :] = p
        return p, r.astype(jnp.bfloat16)

    pr_copies = []
    for part in range(PARTS):
        for way, plane, offset, device, loads in (
            (0, 1, 0, above, first_up),
            (1, 0, half, below, first_down),
        ):
            if part == 0:
                for copy in loads:
                    copy.wait()
            p, r = look_up(plane, offset + part * rows, rows)
            snd[way, part, 0] = p
            snd[way, part, 1] = r
            copy = remote(
                snd.at[way, part],
                rcv.at[way, part],
                pr_send.at[way, part],
                pr_recv.at[way, part],
                device,
            )
            copy.start()
            pr_copies.append(copy)

    for copy in later + tuple(behind):
        copy.wait()

    def rest(step, carry):
        start = pl.multiple_of(step * rows, rows)
        look_up(0, start, rows)
        look_up(1, start + half, rows)
        return carry

    lax.fori_loop(0, PARTS, rest, 0)

    edge = pl.multiple_of(HALO + (1 - bi) * (width_y - 8), 8)
    p_copy = remote(
        pv.at[:, pl.ds(edge, 8), :], p_edge, one_send.at[2], one_recv.at[2], other
    )
    r_copy = remote(
        rv.at[:, pl.ds(edge, 8), :], r_edge, one_send.at[3], one_recv.at[3], other
    )
    p_copy.start()
    r_copy.start()

    y_start = bi * width_y

    def sample(step, carry):
        at = pl.ds(pl.multiple_of(step * F_TILE, F_TILE), F_TILE)
        z = corner[2:3, at]
        fz = fraction[2:3, at]
        iota = lax.broadcasted_iota(jnp.int16, (width_z, F_TILE), 0)
        z = jnp.broadcast_to(z, (16, F_TILE)).astype(jnp.int16)[0:1]
        weight = jnp.where(
            iota == z,
            (1.0 - fz).astype(jnp.bfloat16),
            jnp.where(iota == z + 1, fz.astype(jnp.bfloat16), jnp.bfloat16(0.0)),
        )
        wz[:, at] = weight
        along_z = jnp.dot(p_low[...], weight, preferred_element_type=jnp.float32)
        y = corner[1:2, at] - y_start
        fy = fraction[1:2, at]
        fx = fraction[0:1, at]
        flow = flow_row[:, at]
        iota = lax.broadcasted_iota(jnp.int32, (width_y, F_TILE), 0)
        weight_y = jnp.where(iota == y, 1.0 - fy, jnp.where(iota == y + 1, fy, jnp.float32(0.0)))
        low = jnp.sum(along_z[:width_y] * weight_y, axis=0, keepdims=True)
        high = jnp.sum(along_z[width_y:] * weight_y, axis=0, keepdims=True)
        fp_row[:, at] = (1.0 - fx) * low + fx * high
        wyx[0:width_y, at] = (weight_y * ((1.0 - fx) * flow)).astype(jnp.bfloat16)
        wyx[width_y:, at] = (weight_y * (fx * flow)).astype(jnp.bfloat16)
        return carry

    steps = cells // F_TILE
    lax.fori_loop(0, 1, sample, 0)

    for copy in x_copies:
        copy.wait_recv()
    mine = jnp.concatenate([gather_x[i, 0:4, :] for i in range(nx)], axis=0)
    gather[yi, zi] = mine.astype(jnp.bfloat16)
    z_copies = [
        remote(gather.at[yi, zi], gather.at[yi, zi], z_send.at[d], z_recv.at[d], peer)
        for d, peer in enumerate(z_peers)
    ]
    for copy in z_copies:
        copy.start()

    has_below = jnp.where(slab > 0, 1.0, 0.0).astype(jnp.float32)
    has_above = jnp.where(slab < slabs - 1, 1.0, 0.0).astype(jnp.float32)
    fl_copies = {}

    def faces(part):
        for way, plane, offset, device, present in (
            (0, 0, 0, below, has_below),
            (1, 1, half, above, has_above),
        ):
            pr_copies[2 * part + way].wait_recv()
            at = pl.ds(HALO + offset + part * rows, rows)
            p_in = rcv[way, part, 0].astype(jnp.float32)
            r_in = rcv[way, part, 1].astype(jnp.float32)
            drop = pv[plane, at, :] - p_in
            flux = drop * (inverse(rv[plane, at, :] + r_in) * -present)
            fsnd[way, part] = flux.astype(jnp.bfloat16)
            copy = remote(
                fsnd.at[way, part],
                frcv.at[way, part],
                fl_send.at[way, part],
                fl_recv.at[way, part],
                device,
            )
            copy.start()
            fl_copies[way, part] = copy

    lax.fori_loop(1, 3, sample, 0)
    faces(0)
    lax.fori_loop(3, steps, sample, 0)
    for c in range(16):
        fp_own[c : c + 1, :] = fp_row[:, 128 * c : 128 * (c + 1)]
    fp_copy = remote(fp_own, fp_other, one_send.at[4], one_recv.at[4], other)
    fp_copy.start()

    for copy in z_copies:
        copy.wait_recv()
    y_copies = [
        remote(gather.at[yi], gather.at[yi], y_send.at[d], y_recv.at[d], peer)
        for d, peer in enumerate(y_peers)
    ]
    for copy in y_copies:
        copy.start()

    slip_up.wait_recv()
    slip_down.wait_recv()
    window[0:1, :] = has_below * jnp.concatenate(
        [slip_edge[0, 4 + q : 5 + q, :] for q in range(4)], axis=1
    )
    window[5:6, :] = has_above * jnp.concatenate(
        [slip_edge[1, q : 1 + q, :] for q in range(4)], axis=1
    )
    load_near.wait()
    for i in range(2):
        total = jnp.zeros((8, 512), jnp.float32)
        for j in range(3):
            row = window[pl.ds(2 * bi + i + j, 1), :]
            row = jnp.broadcast_to(row, (8, 512)).astype(jnp.bfloat16)
            total = total + lax.dot_general(
                row, near[i, j], (((1,), (1,)), ((), ())), preferred_element_type=jnp.float32
            )
        store_rows(near_own, 4 * i, total[0:1, :])
    near_copy = remote(near_own, near_other, one_send.at[5], one_recv.at[5], other)
    near_copy.start()
    faces(1)

    p_copy.wait_recv()
    r_copy.wait_recv()
    inner = (1 - bi).astype(jnp.float32)
    for plane in range(planes):
        p_lower, r_lower = p_edge[plane, 7:8, :], r_edge[plane, 7:8, :]
        p_upper, r_upper = p_edge[plane, 0:1, :], r_edge[plane, 0:1, :]
        pv[plane, 7:8, :] = p_lower
        rv[plane, 7:8, :] = r_lower + inner * FAR
        pv[plane, HALO + width_y : HALO + width_y + 1, :] = p_upper
        rv[plane, HALO + width_y : HALO + width_y + 1, :] = r_upper + (1.0 - inner) * FAR

    def stencil(y):
        p = [pv[plane, pl.ds(HALO + y, 8), :] for plane in range(planes)]
        r = [rv[plane, pl.ds(HALO + y, 8), :] for plane in range(planes)]
        last = lax.broadcasted_iota(jnp.int32, (8, width_z), 1) == width_z - 1
        between = (p[1] - p[0]) * inverse(r[0] + r[1])
        for plane in range(planes):
            pc, rc = p[plane], r[plane]
            total = between if plane == 0 else -between
            for shift in (1, -1):
                pn = pv.at[plane, pl.ds(y, 24), :][HALO + shift : HALO + shift + 8, :]
                rn = rv.at[plane, pl.ds(y, 24), :][HALO + shift : HALO + shift + 8, :]
                total = total + (pn - pc) * inverse(rn + rc)
            pn = pltpu.roll(pc, width_z - 1, 1)
            rn = pltpu.roll(rc, width_z - 1, 1)
            flux = jnp.where(last, jnp.float32(0.0), (pn - pc) * inverse(rn + rc))
            total = total + flux - pltpu.roll(flux, 1, 1)
            acc[plane, pl.ds(y, 8), :] = total

    def spread_source(step, carry):
        at = pl.ds(pl.multiple_of(step * Z_TILE, Z_TILE), Z_TILE)
        result = lax.dot_general(
            wyx[...], wz[at, :], (((1,), (1,)), ((), ())), preferred_element_type=jnp.float32
        )
        source[0, :, at] = result[:width_y]
        source[1, :, at] = result[width_y:]
        count = width_y // 8 // (width_z // Z_TILE)
        for k in range(count):
            stencil(pl.multiple_of((step * count + k) * 8, 8))
        return carry

    spreads = width_z // Z_TILE
    lax.fori_loop(0, spreads // 2, spread_source, 0)
    faces(2)
    faces(3)

    for copy in last:
        copy.wait()
    column = lanes_row(far_col, 0, 8)
    pick[...] = jnp.where(
        lax.broadcasted_iota(jnp.int32, pick.shape, 0) == column, 1.0, 0.0
    ).astype(jnp.bfloat16)
    for copy in y_copies:
        copy.wait_recv()
    moments = gather[...].reshape(512, 128)[:, 0:rank]
    picked = lax.dot_general(
        moments, pick[...], (((0,), (0,)), ((), ())), preferred_element_type=jnp.float32
    )
    ranks = lanes_row(far_rank, 0, 8)
    masked = jnp.where(
        lax.broadcasted_iota(jnp.int32, picked.shape, 0) < ranks, picked, jnp.float32(0.0)
    )
    load_coupling.wait()
    for a in range(rank):
        block[a : a + 1, :] = jnp.sum(
            coupling[a].astype(jnp.float32) * masked, axis=0, keepdims=True
        )
    target = lanes_row(far_row, 0, 8)
    lane = lax.broadcasted_iota(jnp.int32, (rank, 128), 1)
    totals = jnp.zeros((rank, 128), jnp.float32)
    for c in range(4):
        share = jnp.sum(
            jnp.where(target == c, block[...], jnp.float32(0.0)), axis=1, keepdims=True
        )
        totals = totals + jnp.where(lane == c, share, jnp.float32(0.0))
    tot_own[...] = totals
    tot_copy = remote(tot_own, tot_other, one_send.at[6], one_recv.at[6], other)
    tot_copy.start()

    lax.fori_loop(spreads // 2, spreads, spread_source, 0)

    stores = []
    for part in range(PARTS):
        low = pl.ds(part * rows, rows)
        high = pl.ds(half + part * rows, rows)
        for which, plane, at, flux in (
            (0, 0, low, fsnd.at[0, part]),
            (1, 1, high, fsnd.at[1, part]),
        ):
            value = flux[...].astype(jnp.float32)
            acc[plane, at, :] = acc[plane, at, :] + source[plane, at, :] + value
            copy = pltpu.make_async_copy(
                acc.at[plane, at], rate_hbm.at[plane, at], out_sem.at[which, part]
            )
            copy.start()
            stores.append(copy)

    tot_copy.wait_recv()
    near_copy.wait_recv()
    fp_copy.wait_recv()
    totals = tot_own[...] + tot_other[...]
    for c in range(4):
        basis = row_basis[:, 512 * c : 512 * (c + 1)].astype(jnp.float32)
        store_rows(
            far16, 4 * c, jnp.sum(basis * totals[:, c : c + 1], axis=0, keepdims=True)
        )
    own, others = near_own[...], near_other[...]
    first = bi == 0
    near16 = jnp.concatenate(
        [jnp.where(first, own, others), jnp.where(first, others, own)], axis=0
    )
    traction = near16 + far16[...]
    effective = stress[...] - (fp_own[...] + fp_other[...])
    rate = slip[...]
    state_rate = jnp.exp(-log_state[...]) - rate
    accel_out[...] = (traction - effective * friction_b[...] * state_rate) / (
        effective * friction_a[...] / rate + 0.5
    )
    state_out[...] = state_rate

    for part in range(PARTS):
        low = pl.ds(part * rows, rows)
        high = pl.ds(half + part * rows, rows)
        for which, plane, at, way in ((2, 1, low, 0), (3, 0, high, 1)):
            fl_copies[way, part].wait_recv()
            value = frcv[way, part].astype(jnp.float32)
            acc[plane, at, :] = acc[plane, at, :] + source[plane, at, :] - value
            copy = pltpu.make_async_copy(
                acc.at[plane, at], rate_hbm.at[plane, at], out_sem.at[which, part]
            )
            copy.start()
            stores.append(copy)
    for copy in stores:
        copy.wait()
    sent = x_copies + z_copies + y_copies + pr_copies + list(fl_copies.values())
    for copy in sent + [slip_up, slip_down, p_copy, r_copy, fp_copy, near_copy, tot_copy]:
        copy.wait_send()


def hand_over(rate_in, accel_in, state_in, rate, accel, state, held, held_two, sem):
    planes, width_y, _ = rate.shape
    part = width_y // 4
    ways = [(accel_in, held_two.at[0], accel), (state_in, held_two.at[1], state)]
    for plane in range(planes):
        for k in range(4):
            at = (plane, pl.ds(part * k, part))
            ways.append((rate_in.at[at], held.at[at], rate.at[at]))
    loads = [
        pltpu.make_async_copy(src, mid, sem.at[0, i]) for i, (src, mid, _) in enumerate(ways)
    ]
    stores = [
        pltpu.make_async_copy(mid, dst, sem.at[1, i]) for i, (_, mid, dst) in enumerate(ways)
    ]
    for load in loads:
        load.start()
    for load, store in zip(loads, stores):
        load.wait()
        store.start()
    for store in stores:
        store.wait()


def shards(
    slip_rate,
    log_state,
    friction_a,
    friction_b,
    normal_stress,
    leak_rate,
    corner,
    fraction,
    near_blocks,
    row_basis,
    col_basis,
    far_row,
    far_col,
    far_rank,
    far_coupling,
    pressure,
    region,
    perm_table,
):
    sizes = tuple(lax.axis_size(name) for name in SLAB)
    ny, nz, nx = sizes
    planes, width_y, width_z = pressure.shape
    cells = slip_rate.shape[0]
    clusters = cells // 512
    slots = far_row.shape[0]
    rank = col_basis.shape[0]
    rows = width_y // 2 // PARTS
    f32, bf16 = jnp.float32, jnp.bfloat16
    vmem = pl.BlockSpec(memory_space=pltpu.VMEM)
    hbm = pl.BlockSpec(memory_space=pl.ANY)
    dma = pltpu.SemaphoreType.DMA

    def cut(x):
        return x.reshape(-1, 128)

    shapes = (
        jax.ShapeDtypeStruct(pressure.shape, f32),
        jax.ShapeDtypeStruct((cells // 128, 128), f32),
        jax.ShapeDtypeStruct((cells // 128, 128), f32),
    )
    results = pl.pallas_call(
        functools.partial(kernel, sizes),
        out_shape=shapes,
        in_specs=[hbm] * 18,
        out_specs=(hbm, vmem, vmem),
        scratch_shapes=[
            *[pltpu.VMEM((cells // 128, 128), f32)] * 6,
            pltpu.VMEM(corner.shape, jnp.int32),
            pltpu.VMEM(fraction.shape, f32),
            pltpu.VMEM(row_basis.shape, bf16),
            pltpu.VMEM(col_basis.shape, bf16),
            *[pltpu.VMEM((slots // 128, 128), jnp.int32)] * 3,
            pltpu.VMEM((1, perm_table.shape[0]), f32),
            pltpu.VMEM((planes, width_y + 2 * HALO, width_z), f32),
            pltpu.VMEM((planes, width_y + 2 * HALO, width_z), f32),
            pltpu.VMEM((planes, width_y, width_z), jnp.int32),
            pltpu.VMEM((planes, width_y, width_z), f32),
            pltpu.VMEM((planes, width_y, width_z), f32),
            pltpu.VMEM((2, PARTS, 2, rows, width_z), bf16),
            pltpu.VMEM((2, PARTS, 2, rows, width_z), bf16),
            pltpu.VMEM((2, PARTS, rows, width_z), bf16),
            pltpu.VMEM((2, PARTS, rows, width_z), bf16),
            pltpu.VMEM((planes, 8, width_z), f32),
            pltpu.VMEM((planes, 8, width_z), f32),
            pltpu.VMEM((width_z, cells), bf16),
            pltpu.VMEM((planes * width_y, cells), bf16),
            pltpu.VMEM((planes * width_y, width_z), bf16),
            pltpu.VMEM(near_blocks.shape, bf16),
            pltpu.VMEM(far_coupling.shape, bf16),
            pltpu.VMEM((ny * nz * nx * clusters, slots), bf16),
            pltpu.VMEM((nx, 8, 128), f32),
            pltpu.VMEM((ny, nz, nx * clusters, 128), bf16),
            pltpu.VMEM((2, 8, 128), f32),
            pltpu.VMEM((8, 512), f32),
            pltpu.VMEM((1, cells), f32),
            pltpu.VMEM((1, cells), f32),
            pltpu.VMEM((cells // 128, 128), f32),
            pltpu.VMEM((cells // 128, 128), f32),
            pltpu.VMEM((8, 128), f32),
            pltpu.VMEM((8, 128), f32),
            pltpu.VMEM((rank, 128), f32),
            pltpu.VMEM((rank, 128), f32),
            pltpu.VMEM((rank, slots), f32),
            pltpu.VMEM((cells // 128, 128), f32),
            dma((24,)),
            dma((nx - 1,)),
            dma((nx - 1,)),
            dma((nz - 1,)),
            dma((nz - 1,)),
            dma((ny - 1,)),
            dma((ny - 1,)),
            dma((2, PARTS)),
            dma((2, PARTS)),
            dma((2, PARTS)),
            dma((2, PARTS)),
            dma((7,)),
            dma((7,)),
            dma((4, PARTS)),
        ],
        compiler_params=pltpu.CompilerParams(
            collective_id=0, has_side_effects=True, vmem_limit_bytes=60 * 1024 * 1024
        ),
        name="fault_step",
    )(
        cut(slip_rate),
        cut(log_state),
        cut(friction_a),
        cut(friction_b),
        cut(normal_stress),
        cut(leak_rate),
        corner,
        fraction,
        row_basis,
        col_basis,
        cut(far_row),
        cut(far_col),
        cut(far_rank),
        perm_table.reshape(1, -1),
        near_blocks,
        far_coupling,
        pressure,
        region,
    )
    rate, accel, state = pl.pallas_call(
        hand_over,
        out_shape=shapes,
        in_specs=[hbm] * 3,
        out_specs=(hbm,) * 3,
        scratch_shapes=[
            pltpu.VMEM(pressure.shape, f32),
            pltpu.VMEM((2, cells // 128, 128), f32),
            dma((2, 10)),
        ],
        compiler_params=pltpu.CompilerParams(vmem_limit_bytes=60 * 1024 * 1024),
        name="hand_over",
    )(*results)
    return accel.reshape(cells), state.reshape(cells), rate


def solution(mesh):
    torus = Mesh(
        mesh.devices.reshape(4, 8, 4, mesh.shape["blk"]), ("slab_0", "slab_1", "slab_2", "blk")
    )
    placed = (
        P(SLAB),
        P(SLAB),
        P(SLAB),
        P(SLAB),
        P(SLAB),
        P(SLAB),
        P(None, SLAB),
        P(None, SLAB),
        P(SLAB_BLK, None, None, None),
        P(None, SLAB),
        P(None, SLAB),
        P(SLAB_BLK),
        P(SLAB_BLK),
        P(SLAB_BLK),
        P(None, None, SLAB_BLK),
        P(SLAB, "blk", None),
        P(SLAB, "blk", None),
        P(),
    )
    return jax.shard_map(
        shards,
        mesh=torus,
        in_specs=placed,
        out_specs=(P(SLAB), P(SLAB), P(SLAB, "blk", None)),
        check_vma=False,
    )
```
